256 devices in a mesh: img: 32 (over x, z), txt: 8 (over y, core).
Axes of the slice: x: 4, y: 4, z: 8, core: 2. Of those that a mesh axis runs over, the one named last changes fastest.
Arguments:
- image_emb: bfloat16 [16384, 1152], P(('img', 'txt')), may hold values from -6 to 6
- text_emb: bfloat16 [16384, 1152], P(('txt', 'img')), may hold values from -6 to 6
- log_scale: float32 [1], replicated, may hold values from 1.6 to 2.7
- bias: float32 [1], replicated, may hold values from -4 to -1
Outputs:
- loss: float32 [1], replicated
- image_grad: float32 [16384, 1152], P(('img', 'txt'))
- text_grad: float32 [16384, 1152], P(('txt', 'img'))
The draws below stay inside these ranges and needn't reach their ends.
All inputs are finite; a program needn't handle non-finite values.
Results may differ from the reference program's by a relative error of at most 0.0007.
The reference program's roundings to bfloat16 on the way (of `image_unit`, `text_unit` and `coef`) count: a program that leaves them out, or rounds other values in their place, can miss the bound.
Values may be sent and summed in bfloat16 or wider, within the bound.
A program may use at most 64 MiB of HBM per device.

```python
import math
import jax
import jax.numpy as jnp
from jax import lax

D = 1152
TOKENS = 16384


def shard_levels(stream_key, dims, cuts, least, top_value):
    def one(axis_at, blocks):
        heights = jax.random.uniform(jax.random.fold_in(jax.random.fold_in(stream_key, 6), axis_at), (blocks,), jnp.float32, least / len(cuts), top_value / len(cuts))
        return jnp.repeat(jnp.exp(heights), dims[axis_at] // blocks).reshape((-1,) + (1,) * (len(dims) - axis_at - 1))

    factor_of = one(*cuts[0])
    for cut in cuts[1:]:
        factor_of = factor_of * one(*cut)
    return factor_of


def normal_values(rng, shape, scale, bound, cuts=(), kind=jnp.bfloat16):
    array = scale * jax.random.normal(rng, shape, jnp.float32)
    if cuts:
        array = array * shard_levels(rng, shape, cuts, -0.22, 0.18)
    return jnp.clip(array, -bound, bound).astype(kind)


def setup_inputs(seed: int = 0) -> dict:
    streams_of = jax.random.split(jax.random.key(seed), 5)
    image_emb = normal_values(streams_of[0], (TOKENS, D), 1.0, 6.0, ((0, 256),))
    text_emb = normal_values(streams_of[1], (TOKENS, D), 1.0, 6.0, ((0, 256),))
    log_scale = jnp.clip(jax.random.uniform(streams_of[2], (1,), jnp.float32, 1.6, 2.7), 1.6, 2.7)
    bias = jnp.clip(jax.random.uniform(streams_of[3], (1,), jnp.float32, -4.0, -1.0), -4.0, -1.0)
    return {"image_emb": image_emb, "text_emb": text_emb, "log_scale": log_scale, "bias": bias}


def normalize(values):
    wide = values.astype(jnp.float32)
    norm = jnp.sqrt(lax.optimization_barrier(jnp.sum(wide * wide, axis=1, keepdims=True)) + 1e-06)
    direction = wide / norm
    return (norm, direction, direction.astype(jnp.bfloat16))

def project_back(dgrad, direction, norm):
    along = lax.optimization_barrier(jnp.sum(direction * dgrad, axis=1, keepdims=True))
    return (dgrad - direction * along) / norm

def reference(image_emb, text_emb, log_scale, bias):
    total = image_emb.shape[0]
    width = image_emb.shape[1]
    scale = jnp.exp(log_scale[0])
    offset = bias[0]
    image_norm, image_dir, image_unit = normalize(image_emb)
    text_norm, text_dir, text_unit = normalize(text_emb)
    block = math.gcd(total, 512)
    count = total // block
    col_ids = jnp.arange(total, dtype=jnp.int32)

    def one_block(carry, index):
        text_acc, loss_acc = carry
        start = (index * block).astype(jnp.int32)
        rows = lax.dynamic_slice_in_dim(image_unit, start, block, 0)
        row_ids = start + jnp.arange(block, dtype=jnp.int32)
        logits = scale * jnp.dot(rows, text_unit.T, preferred_element_type=jnp.float32) + offset
        label = jnp.where(row_ids[:, None] == col_ids[None, :], 1.0, -1.0).astype(jnp.float32)
        loss_acc = loss_acc + jnp.sum(jnp.logaddexp(0.0, -label * logits))
        coef = (-label * jax.nn.sigmoid(-label * logits) * scale).astype(jnp.bfloat16)
        image_part = jnp.dot(coef, text_unit, preferred_element_type=jnp.float32)
        text_acc = text_acc + lax.dot_general(coef, rows, (((0,), (0,)), ((), ())), preferred_element_type=jnp.float32)
        return ((text_acc, loss_acc), image_part)
    start_carry = (jnp.zeros((total, width), jnp.float32), jnp.zeros((), jnp.float32))
    (text_dgrad, loss_sum), image_parts = lax.scan(one_block, start_carry, jnp.arange(count, dtype=jnp.int32))
    image_dgrad = image_parts.reshape(total, width)
    loss = (loss_sum / total).reshape(1)
    return (loss, project_back(image_dgrad, image_dir, image_norm), project_back(text_dgrad, text_dir, text_norm))
```

```python
import functools
import heapq

import jax
import jax.numpy as jnp
from jax import lax
from jax.experimental import pallas as pl
from jax.experimental.pallas import tpu as pltpu
from jax.sharding import PartitionSpec as P

F32 = jnp.float32
BF16 = jnp.bfloat16
MESH = pl.DeviceIdType.MESH
NT = (((1,), (1,)), ((), ()))
TN = (((0,), (0,)), ((), ()))
TOTAL = 16384
LOG2E = 1.4426950408889634
POWER = 7

ROW_US = 0.049
HOP_US = 2.0
CORE_ROW_US = 0.005
CORE_HOP_US = 1.0


def encode(v):
    v2 = v * v
    return (v2 * v2 * v2 * v).astype(BF16)


def decode(w):
    w = w.astype(F32)
    m = jnp.exp2(jnp.log2(jnp.abs(w)) * (1.0 / POWER))
    return jnp.where(w < 0.0, -m, m)


class Plan:
    def __init__(self):
        self.tasks = []
        self.sends = {}

    def send(self, event, link, rows, wire=True):
        if link == "c":
            self.sends[event] = (link, rows * CORE_ROW_US, CORE_HOP_US)
        else:
            self.sends[event] = (link, rows * ROW_US, HOP_US)
        return event

    def task(self, name, deps, cost, fn, sends=(), rank=0):
        self.tasks.append((name, tuple(deps), cost, fn, tuple(sends), rank))

    def order(self):
        done, free = {}, {}
        left = list(self.tasks)
        now, out = 0.0, []
        while left:
            best = None
            for i, (name, deps, cost, fn, sends, rank) in enumerate(left):
                if any(d not in done for d in deps):
                    continue
                ready = max([done[d] for d in deps], default=0.0)
                key = (max(ready, now), rank, ready, i)
                if best is None or key < best[0]:
                    best = (key, i)
            (start, _, _, _), i = best
            name, deps, cost, fn, sends, rank = left.pop(i)
            now = start + cost
            done[name] = now
            for event in sends:
                link, wire, hop = self.sends[event]
                begin = max(now, free.get(link, 0.0))
                free[link] = begin + wire
                done[event] = begin + wire + hop
            out.append((name, deps, fn, start))
        self.span = now
        return out


def kernel(
    img_ref, txt_ref, scale_ref, bias_ref, loss_ref, igrad_ref, tgrad_ref,
    IR, TR, CF, QI, OI, DI, TP, ZS, ZR, YS, YR, LS, LC, LX, LY, LZ, send_sem, recv_sem,
):
    img, txt = lax.axis_index("img"), lax.axis_index("txt")
    x, z, y, c = img // 8, img % 8, txt // 2, txt % 2

    def device(dx=0, dy=0, dz=0, dc=0):
        return (
            lax.rem(x + dx + 4, 4) * 8 + lax.rem(z + dz + 8, 8),
            lax.rem(y + dy + 4, 4) * 2 + lax.rem(c + dc, 2),
        )

    ways = {
        "x+": device(dx=1), "x-": device(dx=-1), "y+": device(dy=1), "y-": device(dy=-1),
        "z+": device(dz=1), "z-": device(dz=-1), "c": device(dc=1),
    }
    far = {("x", k): device(dx=k) for k in range(1, 4)}
    far |= {("y", k): device(dy=k) for k in range(1, 4)}
    far |= {("z", k): device(dz=k) for k in range(1, 8)}

    barrier = pltpu.get_barrier_semaphore()
    greeted = [ways["c"], *far.values()]
    for peer in greeted:
        pl.semaphore_signal(barrier, inc=1, device_id=peer, device_id_type=MESH)

    scale = jnp.exp(jnp.full((1, 1), scale_ref[0], F32))
    offset = jnp.full((1, 1), bias_ref[0], F32)

    def norm_of(ref):
        wide = ref[...].astype(F32)
        norm = jnp.sqrt(jnp.sum(wide * wide, axis=1, keepdims=True) + 1e-06)
        return wide, norm

    wide, norm = norm_of(img_ref)
    IR[0:64, :] = (wide / norm).astype(BF16)
    wide, norm = norm_of(txt_ref)
    TR[0:64, :] = (wide / norm).astype(BF16)
    LS[...] = jnp.zeros_like(LS)
    pl.semaphore_wait(barrier, len(greeted))

    plan = Plan()
    copies = {}

    def start(event, link, src, dst):
        peer = ways[link] if isinstance(link, str) else far[link]
        index = len(copies)
        copy = pltpu.make_async_remote_copy(
            src_ref=src, dst_ref=dst, send_sem=send_sem.at[index], recv_sem=recv_sem.at[index],
            device_id=peer, device_id_type=MESH,
        )
        copy.start()
        copies[event] = copy

    def forward(name, deps, cost, moves):
        def run():
            for event, link, ref, here, there, rows in moves:
                start(event, link, ref.at[pl.ds(here, rows)], ref.at[pl.ds(there, rows)])

        for event, link, ref, here, there, rows in moves:
            plan.send(event, link, rows)
        plan.task(name, deps, cost, run, [m[0] for m in moves], rank=-1)

    def islot(dz, p):
        return dz * 128 + p * 32

    def image_move(dz, p, way):
        to = (dz - 1) % 8 if way == "z+" else (dz + 1) % 8
        return (("I", to, p), way, IR, islot(dz, p), islot(to, p), 32)

    def tslot(dx, dy, half, q=0):
        return (dx * 4 + dy) * 64 + half * 32 + q * 16

    def text_move(dx, dy, half, way, q=None):
        ex, ey = dx, dy
        if way[0] == "x":
            ex = (dx - 1) % 4 if way == "x+" else (dx + 1) % 4
        else:
            ey = (dy - 1) % 4 if way == "y+" else (dy + 1) % 4
        rows = 32 if q is None else 16
        return (
            ("T", ex, ey, half, q), way, TR,
            tslot(dx, dy, half, q or 0), tslot(ex, ey, half, q or 0), rows,
        )

    first = [image_move(0, 0, "z+"), image_move(0, 0, "z-")]
    first += [text_move(0, 0, 0, "x+"), text_move(0, 0, 0, "x-")]
    first += [text_move(0, 0, 1, "y+"), text_move(0, 0, 1, "y-")]
    first += [text_move(0, 0, 0, "y+"), text_move(0, 0, 0, "y-")]
    first += [text_move(0, 0, 1, "x+"), text_move(0, 0, 1, "x-")]
    first += [image_move(0, 1, "z+"), image_move(0, 1, "z-")]
    first += [(("J", 0), "c", IR, 0, 64, 64)]
    forward("first", [], 0.3, first)
    for p in range(2):
        for dz in (7, 6, 5):
            if dz != 5 or p == 0:
                forward(("fI", dz, p), [("I", dz, p)], 0.05, [image_move(dz, p, "z+")])
        for dz in (1, 2, 3):
            if dz != 3 or p == 1:
                forward(("fI", dz, p), [("I", dz, p)], 0.05, [image_move(dz, p, "z-")])
    for dz in range(1, 8):
        forward(
            ("fJ", dz), [("I", dz, 0), ("I", dz, 1)], 0.05,
            [(("J", dz), "c", IR, dz * 128, dz * 128 + 64, 64)],
        )
    text_parts = {}
    for half in range(2):
        one, two = ("x", "y") if half == 0 else ("y", "x")

        def at(a, b):
            return (a, b) if half == 0 else (b, a)

        def ev(a, b, q=None):
            return ("T", *at(a, b), half, q)

        def mv(a, b, way, q=None):
            return text_move(*at(a, b), half, way, q)

        forward(
            ("f1", half, 3), [ev(3, 0)], 0.1,
            [mv(3, 0, two + "+"), mv(3, 0, two + "-"), mv(3, 0, one + "+", 0)],
        )
        forward(
            ("f1", half, 1), [ev(1, 0)], 0.1,
            [mv(1, 0, two + "+"), mv(1, 0, two + "-"), mv(1, 0, one + "-", 1)],
        )
        for q in range(2):
            forward(
                ("f1", half, 2, q), [ev(2, 0, q)], 0.1,
                [mv(2, 0, two + "+", q), mv(2, 0, two + "-", q)],
            )
        for a in (0, 3, 1):
            forward(("f2", half, a, 3), [ev(a, 3)], 0.05, [mv(a, 3, two + "+", 0)])
            forward(("f2", half, a, 1), [ev(a, 1)], 0.05, [mv(a, 1, two + "-", 1)])
        forward(("f2", half, 2, 3), [ev(2, 3, 0)], 0.05, [mv(2, 3, two + "+", 0)])
        forward(("f2", half, 2, 1), [ev(2, 1, 1)], 0.05, [mv(2, 1, two + "-", 1)])
        for a in range(4):
            for b in range(4):
                whole = not (a == 2 or b == 2)
                names = [ev(a, b)] if whole else [ev(a, b, 0), ev(a, b, 1)]
                if (a, b) == (0, 0):
                    names = []
                text_parts[(*at(a, b), half)] = names
    image_parts = {dz: [("I", dz, 0), ("I", dz, 1), ("J", dz)] for dz in range(8)}
    image_parts[0] = [("J", 0)]

    def coef_block(r0, c0):
        acc = lax.dot_general(
            IR[r0 : r0 + 256, :], TR[c0 : c0 + 256, :], NT, preferred_element_type=F32
        )
        e = jnp.exp2(acc * (scale * LOG2E) + offset * LOG2E)
        d = 1.0 + e
        r = pltpu.reciprocal(d, approx=True)
        r = r * (2.0 - d * r)
        CF[r0 : r0 + 256, c0 : c0 + 256] = ((e * scale) * r).astype(BF16)
        q = e[:, :128] * d[:, 128:] + e[:, 128:]
        q = q[:128] * (1.0 + q[128:]) + q[128:]
        u = 1.0 + q
        term = jnp.log(u) + (q - (u - 1.0)) * pltpu.reciprocal(u, approx=True)
        LS[...] += jnp.sum(term.reshape(16, 8, 128), axis=0)

    def diagonal():
        @pl.when(y == z // 2)
        def _():
            for other in range(4):
                pair = c * 4 + other
                dz = lax.rem(pair - z + 8, 8)
                core = lax.rem(z + c, 2)
                dx = lax.rem(other - x + 4, 4)
                dy = lax.rem(x - y + 4, 4)
                r0 = pl.multiple_of(dz * 128 + core * 64, 64)
                slot = dx * 4 + dy
                c0 = pl.multiple_of((slot // 2) * 128, 128)
                shift = lax.rem(slot, 2) * 64
                acc = lax.dot_general(
                    IR[pl.ds(r0, 64), :], TR[pl.ds(c0, 128), :], NT, preferred_element_type=F32
                )
                logit = acc * scale + offset
                rows = lax.broadcasted_iota(jnp.int32, (64, 128), 0)
                cols = lax.broadcasted_iota(jnp.int32, (64, 128), 1)
                same = cols == rows + shift
                e = jnp.exp(logit)
                mine = (-scale / (1.0 + e)).astype(BF16)
                block = CF[pl.ds(r0, 64), pl.ds(c0, 128)]
                CF[pl.ds(r0, 64), pl.ds(c0, 128)] = jnp.where(
                    same, mine.astype(F32), block.astype(F32)
                ).astype(BF16)
                less = jnp.where(same, logit, 0.0)
                LS[...] -= jnp.sum(less.reshape(8, 8, 128), axis=0)

    blocks = []
    for pair in (0, 3, 1, 2):
        for dx in (0, 1, 3, 2):
            deps = image_parts[2 * pair] + image_parts[2 * pair + 1]
            for dy in range(4):
                deps = deps + text_parts[dx, dy, 0] + text_parts[dx, dy, 1]
            name = ("coef", pair, dx)
            blocks.append(name)
            plan.task(
                name, ["first", *deps], 0.35,
                functools.partial(coef_block, pair * 256, dx * 256), rank=1,
            )
    plan.task("diag", blocks, 0.2, diagonal, rank=0)

    def spread(name, dep, value, box, place, links, events):
        def run():
            box[pl.ds(place, 1)] = value().reshape(1, 8, 128)
            for link, event in zip(links, events):
                start(event, link, box.at[pl.ds(place, 1)], box.at[pl.ds(place, 1)])

        for link, event in zip(links, events):
            plan.sends[event] = ("tiny", 0.0, 3.5)
        plan.task(name, dep, 0.1, run, events, rank=-1)

    spread("loss0", ["diag"], lambda: LS[...], LC, c, ["c"], [("Lc", 1)])
    dep = [("Lc", 1)]
    for name, box, before, place, span in (("x", LX, LC, x, 4), ("y", LY, LX, y, 4), ("z", LZ, LY, z, 8)):
        links = [(name, k) for k in range(1, span)]
        events = [("L" + name, k) for k in range(1, span)]
        spread("loss" + name, dep, functools.partial(lambda b: jnp.sum(b[...], axis=0), before), box, place, links, events)
        dep = events

    def loss_end():
        loss_ref[0] = jnp.sum(jnp.sum(LZ[...], axis=0)) * (1.0 / TOTAL)

    plan.task("loss", dep, 0.2, loss_end, rank=0)

    def image_group(pair):
        part = jnp.dot(
            CF[pair * 256 : pair * 256 + 256, :], TR[...], preferred_element_type=F32
        )
        for k in range(2):
            dz = 2 * pair + k
            QI[dz * 64 : dz * 64 + 64, :] = part[k * 128 : k * 128 + 64]
            OI[dz * 64 : dz * 64 + 64, :] = part[k * 128 + 64 : k * 128 + 128]
            rows = pl.ds(dz * 64, 64)
            start(("D", dz), "c", OI.at[rows], DI.at[rows])

    def text_group(dx):
        TP[dx * 256 : dx * 256 + 256, :] = lax.dot_general(
            CF[:, dx * 256 : dx * 256 + 256], IR[...], TN, preferred_element_type=F32
        )

    for dz in range(8):
        plan.send(("D", dz), "c", 128)
    for pair, dx in ((2, 2), (1, 1), (3, 3), (0, 0)):
        plan.task(
            ("G", pair), ["diag"], 0.95, functools.partial(image_group, pair),
            [("D", 2 * pair), ("D", 2 * pair + 1)], rank=1,
        )
        plan.task(("TG", dx), ["diag"], 0.95, functools.partial(text_group, dx), rank=1)

    zplace = {}

    def zbox(box, way, dz, p):
        i = zplace.setdefault((way, dz, p), len(zplace))
        return box.at[pl.ds(i * 32, 32)]

    def image_step(way, dz, p, arrived):
        rows = slice(dz * 64 + p * 32, dz * 64 + p * 32 + 32)
        v = QI[rows, :] + DI[rows, :]
        if arrived:
            before = dz + 1 if way == "z+" else dz - 1
            v = v + decode(zbox(ZR, way, before, p)[...])
        zbox(ZS, way, dz, p)[...] = encode(v)
        start(("R", way, dz, p), way, zbox(ZS, way, dz, p), zbox(ZR, way, dz, p))

    for way, places in (("z+", (4, 3, 2, 1)), ("z-", (4, 5, 6, 7))):
        for at_step, dz in enumerate(places):
            for p in range(2):
                keep = 0 if way == "z+" else 1
                if at_step == 0 and p != keep:
                    continue
                arrived = at_step > 1 or (at_step == 1 and p == keep)
                deps = [("G", dz // 2), ("D", dz)]
                if arrived:
                    deps.append(("R", way, places[at_step - 1], p))
                event = plan.send(("R", way, dz, p), way, 32)
                plan.task(
                    ("step", way, dz, p), deps, 0.12,
                    functools.partial(image_step, way, dz, p, arrived), [event], rank=-1,
                )

    def project(emb_ref, rows, dgrad, out_ref):
        wide = emb_ref[rows, :].astype(F32)
        norm = jnp.sqrt(jnp.sum(wide * wide, axis=1, keepdims=True) + 1e-06)
        direction = wide / norm
        along = jnp.sum(direction * dgrad, axis=1, keepdims=True)
        out_ref[rows, :] = (dgrad - direction * along) / norm

    def image_end(p):
        rows = slice(p * 32, p * 32 + 32)
        v = QI[rows, :] + DI[rows, :]
        v = v + decode(zbox(ZR, "z+", 1, p)[...]) + decode(zbox(ZR, "z-", 7, p)[...])
        project(img_ref, rows, v, igrad_ref)

    for p in range(2):
        plan.task(
            ("image_end", p), [("G", 0), ("D", 0), ("R", "z+", 1, p), ("R", "z-", 7, p)], 0.25,
            functools.partial(image_end, p), rank=0,
        )

    place = {}

    def ybox(box, key, rows):
        if key not in place:
            place[key] = sum(r for _, r in place.values()), rows
        return box.at[pl.ds(place[key][0], rows)]

    def put(event, way, v, rows):
        ybox(YS, event, rows)[...] = encode(v)
        start(event, way, ybox(YS, event, rows), ybox(YR, event, rows))

    def take(event, rows):
        return decode(ybox(YR, event, rows)[...])

    for half in range(2):
        one, two = ("y", "x") if half == 0 else ("x", "y")

        def rows_of(a, b, q=None, half=half):
            s = tslot(b, a, half) if half == 0 else tslot(a, b, half)
            if q is None:
                return slice(s, s + 32)
            return slice(s + 16 * q, s + 16 * q + 16)

        def group(a, b, half=half):
            return ("TG", b if half == 0 else a)

        def opening(b, half=half, one=one, rows_of=rows_of):
            put(("U", half, b, 1), one + "+", TP[rows_of(2, b, 0), :], 16)
            put(("U", half, b, 3), one + "-", TP[rows_of(2, b, 1), :], 16)

        def middle(b, a, half=half, one=one, rows_of=rows_of):
            q = 0 if a == 1 else 1
            rows = rows_of(a, b, q)
            TP[rows, :] = TP[rows, :] + take(("U", half, b, a), 16)
            way = one + ("+" if a == 1 else "-")
            put(("U", half, b, 0, a), way, TP[rows_of(a, b), :], 32)

        def joined(b, half=half, rows_of=rows_of):
            return TP[rows_of(0, b), :] + take(("U", half, b, 0, 1), 32) + take(("U", half, b, 0, 3), 32)

        def second(half=half, two=two, joined=joined):
            v = joined(2)
            put(("V", half, 1), two + "+", v[:16], 16)
            put(("V", half, 3), two + "-", v[16:], 16)

        def third(b, half=half, two=two, joined=joined, rows_of=rows_of):
            rows = rows_of(0, b)
            TP[rows, :] = joined(b)
            q = 0 if b == 1 else 1
            part = rows_of(0, b, q)
            TP[part, :] = TP[part, :] + take(("V", half, b), 16)
            way = two + ("+" if b == 1 else "-")
            put(("V", half, 0, b), way, TP[rows, :], 32)

        def end(half=half, joined=joined):
            v = joined(0) + take(("V", half, 0, 1), 32) + take(("V", half, 0, 3), 32)
            project(txt_ref, slice(half * 32, half * 32 + 32), v, tgrad_ref)

        for b in (2, 1, 3, 0):
            events = [
                plan.send(("U", half, b, 1), one + "+", 16),
                plan.send(("U", half, b, 3), one + "-", 16),
            ]
            plan.task(
                ("open", half, b), [group(2, b)], 0.1,
                functools.partial(opening, b), events, rank=-1,
            )
            for a, way in ((1, one + "+"), (3, one + "-")):
                event = plan.send(("U", half, b, 0, a), way, 32)
                plan.task(
                    ("mid", half, b, a), [group(a, b), ("U", half, b, a)], 0.15,
                    functools.partial(middle, b, a), [event], rank=-1,
                )
        base = {b: [group(0, b), ("U", half, b, 0, 1), ("U", half, b, 0, 3)] for b in range(4)}
        events = [
            plan.send(("V", half, 1), two + "+", 16),
            plan.send(("V", half, 3), two + "-", 16),
        ]
        plan.task(("second", half), base[2], 0.2, second, events, rank=-2)
        for b, way in ((1, two + "+"), (3, two + "-")):
            event = plan.send(("V", half, 0, b), way, 32)
            plan.task(
                ("third", half, b), [*base[b], ("V", half, b)], 0.25,
                functools.partial(third, b), [event], rank=-2,
            )
        plan.task(
            ("text_end", half), [*base[0], ("V", half, 0, 1), ("V", half, 0, 3)], 0.3, end, rank=0
        )

    landed = set()

    def land(event):
        if event in plan.sends and event not in landed:
            copies[event].wait_recv()
            landed.add(event)

    for name, deps, fn, _ in plan.order():
        for event in deps:
            land(event)
        fn()
    for event in copies:
        land(event)
    for copy in copies.values():
        copy.wait_send()


def per_device(image_emb, text_emb, log_scale, bias):
    width = image_emb.shape[1]
    vmem = pl.BlockSpec(memory_space=pltpu.VMEM)
    smem = pl.BlockSpec(memory_space=pltpu.SMEM)
    ring = 14 * 32
    return pl.pallas_call(
        kernel,
        out_shape=(
            jax.ShapeDtypeStruct((1,), F32),
            jax.ShapeDtypeStruct((64, width), F32),
            jax.ShapeDtypeStruct((64, width), F32),
        ),
        in_specs=[vmem, vmem, smem, smem],
        out_specs=(smem, vmem, vmem),
        scratch_shapes=[
            pltpu.VMEM((1024, width), BF16),
            pltpu.VMEM((1024, width), BF16),
            pltpu.VMEM((1024, 1024), BF16),
            pltpu.VMEM((512, width), F32),
            pltpu.VMEM((512, width), F32),
            pltpu.VMEM((512, width), F32),
            pltpu.VMEM((1024, width), F32),
            pltpu.VMEM((ring, width), BF16),
            pltpu.VMEM((ring, width), BF16),
            pltpu.VMEM((960, width), BF16),
            pltpu.VMEM((960, width), BF16),
            pltpu.VMEM((8, 128), F32),
            pltpu.VMEM((2, 8, 128), F32),
            pltpu.VMEM((4, 8, 128), F32),
            pltpu.VMEM((4, 8, 128), F32),
            pltpu.VMEM((8, 8, 128), F32),
            pltpu.SemaphoreType.DMA((160,)),
            pltpu.SemaphoreType.DMA((160,)),
        ],
        compiler_params=pltpu.CompilerParams(
            collective_id=0, has_side_effects=True, vmem_limit_bytes=56 << 20
        ),
        cost_estimate=pl.CostEstimate(
            flops=6 * 1024 * 1024 * width, bytes_accessed=64 * width * 12, transcendentals=1 << 22
        ),
    )(image_emb, text_emb, log_scale, bias)


def solution(mesh):
    in_specs = (P(("img", "txt"), None), P(("txt", "img"), None), P(), P())
    out_specs = (P(), P(("img", "txt"), None), P(("txt", "img"), None))
    return jax.shard_map(
        per_device, mesh=mesh, in_specs=in_specs, out_specs=out_specs, check_vma=False
    )
```

```python
import functools

import jax
import jax.numpy as jnp
from jax import lax
from jax.experimental import pallas as pl
from jax.experimental.pallas import tpu as pltpu
from jax.sharding import PartitionSpec as P

F32 = jnp.float32
BF16 = jnp.bfloat16
MESH = pl.DeviceIdType.MESH
NT = (((1,), (1,)), ((), ()))
TN = (((0,), (0,)), ((), ()))
TOTAL = 16384
LOG2E = 1.4426950408889634

CHUNKS = (
    (2, 2), (2, 1), (2, 3), (1, 2),
    (3, 2), (2, 0), (0, 2), (1, 1),
    (1, 3), (3, 1), (3, 3), (1, 0),
    (3, 0), (0, 1), (0, 3), (0, 0),
)
PLACE = {chunk: i for i, chunk in enumerate(CHUNKS)}
POWER = 7

ROW_US = 0.049
HOP_US = 2.3
FAR_US = 2.7
CORE_ROW_US = 0.005
CORE_HOP_US = 1.0


def encode(v):
    v2 = v * v
    return (v2 * v2 * v2 * v).astype(BF16)


def decode(w):
    w = w.astype(F32)
    m = jnp.exp2(jnp.log2(jnp.abs(w)) * (1.0 / POWER))
    return jnp.where(w < 0.0, -m, m)


class Plan:
    def __init__(self):
        self.tasks = []
        self.sends = {}

    def send(self, event, link, rows):
        if link == "c":
            self.sends[event] = (("c",), rows * CORE_ROW_US, CORE_HOP_US)
        elif link == "tiny":
            self.sends[event] = ((), 0.0, 4.0)
        elif link[1] == "2":
            self.sends[event] = ((link[0] + "+", link[0] + "-"), rows * ROW_US, FAR_US)
        else:
            self.sends[event] = ((link,), rows * ROW_US, HOP_US)
        return event

    def task(self, name, deps, cost, fn, sends=()):
        self.tasks.append((name, tuple(deps), cost, fn, tuple(sends)))

    def levels(self):
        users, maker = {}, {}
        for i, (name, deps, _, _, sends) in enumerate(self.tasks):
            maker[name] = i
            for d in deps:
                users.setdefault(d, []).append(i)
        level = {}

        def of(i):
            if i not in level:
                name, _, cost, _, sends = self.tasks[i]
                after = [of(j) for j in users.get(name, ())]
                for e in sends:
                    _, wire, hop = self.sends[e]
                    after += [wire + hop + of(j) for j in users.get(e, ())]
                level[i] = cost + max(after, default=0.0)
            return level[i]

        return [of(i) for i in range(len(self.tasks))]

    def order(self):
        level = self.levels()
        done, free, out = {}, {}, []
        left = list(range(len(self.tasks)))
        now = 0.0
        while left:
            best = None
            for i in left:
                deps = self.tasks[i][1]
                if any(d not in done for d in deps):
                    continue
                ready = max([done[d] for d in deps], default=0.0)
                key = (max(ready, now), -level[i], i)
                if best is None or key < best:
                    best = key
            start, _, i = best
            left.remove(i)
            name, deps, cost, fn, sends = self.tasks[i]
            now = start + cost
            done[name] = now
            for event in sends:
                links, wire, hop = self.sends[event]
                begin = max([now, *(free.get(link, 0.0) for link in links)])
                for link in links:
                    free[link] = begin + wire
                done[event] = begin + wire + hop
            out.append((name, deps, fn, start))
        self.span = now
        return out


def kernel(
    img_hbm, txt_hbm, scale_ref, bias_ref, loss_ref, igrad_ref, tgrad_ref,
    IR, TR, CF, QI, OI, DI, TP, ZS, ZR, YS, YR, LS, LC, LX, LY, LZ, img_ref, txt_ref,
    send_sem, recv_sem, in_sem,
):
    img, txt = lax.axis_index("img"), lax.axis_index("txt")
    x, z, y, c = img // 8, img % 8, txt // 2, txt % 2

    def device(dx=0, dy=0, dz=0, dc=0):
        return (
            lax.rem(x + dx + 4, 4) * 8 + lax.rem(z + dz + 8, 8),
            lax.rem(y + dy + 4, 4) * 2 + lax.rem(c + dc, 2),
        )

    ways = {
        "x+": device(dx=1), "x-": device(dx=-1), "y+": device(dy=1), "y-": device(dy=-1),
        "z+": device(dz=1), "z-": device(dz=-1), "c": device(dc=1),
        "x2": device(dx=2), "y2": device(dy=2),
    }
    far = {("x", k): device(dx=k) for k in range(1, 4)}
    far |= {("y", k): device(dy=k) for k in range(1, 4)}
    far |= {("z", k): device(dz=k) for k in range(1, 8)}

    barrier = pltpu.get_barrier_semaphore()
    greeted = list(ways.values())
    for peer in greeted:
        pl.semaphore_signal(barrier, inc=1, device_id=peer, device_id_type=MESH)
    inputs = [
        pltpu.make_async_copy(img_hbm, img_ref, in_sem.at[0]),
        pltpu.make_async_copy(txt_hbm, txt_ref, in_sem.at[1]),
    ]
    for copy in inputs:
        copy.start()

    scale = jnp.exp(jnp.full((1, 1), scale_ref[0], F32))
    offset = jnp.full((1, 1), bias_ref[0], F32)

    def unit(ref):
        wide = ref[...].astype(F32)
        norm = jnp.sqrt(jnp.sum(wide * wide, axis=1, keepdims=True) + 1e-06)
        return (wide / norm).astype(BF16)

    LS[...] = jnp.zeros_like(LS)
    inputs[0].wait()
    IR[0:64, :] = unit(img_ref)
    inputs[1].wait()
    TR[960:1024, :] = unit(txt_ref)
    pl.semaphore_wait(barrier, len(greeted))

    plan = Plan()
    copies = {}

    def start(event, link, src, dst):
        peer = ways[link] if isinstance(link, str) else far[link]
        index = len(copies)
        copy = pltpu.make_async_remote_copy(
            src_ref=src, dst_ref=dst, send_sem=send_sem.at[index], recv_sem=recv_sem.at[index],
            device_id=peer, device_id_type=MESH,
        )
        copy.start()
        copies[event] = copy

    def forward(name, deps, moves):
        def run():
            for event, link, ref, here, there, rows in moves:
                start(event, link, ref.at[pl.ds(here, rows)], ref.at[pl.ds(there, rows)])

        for event, link, _, _, _, rows in moves:
            plan.send(event, link, rows)
        plan.task(name, deps, 0.02 + 0.03 * len(moves), run, [m[0] for m in moves])

    def islot(dz, p):
        return dz * 128 + p * 16

    def image_move(dz, p, way):
        to = (dz - 1) % 8 if way == "z+" else (dz + 1) % 8
        return (("I", to, p), way, IR, islot(dz, p), islot(to, p), 16)

    def tslot(dx, dy, half, q=0):
        return PLACE[dx, dy] * 64 + half * 32 + q * 16

    def text_move(dx, dy, half, way, q):
        step = {"+": -1, "-": 1, "2": 2}[way[1]]
        ex = (dx + step) % 4 if way[0] == "x" else dx
        ey = (dy + step) % 4 if way[0] == "y" else dy
        event = ("T", ex, ey, half, q)
        return (event, way, TR, tslot(dx, dy, half, q), tslot(ex, ey, half, q), 16)

    first = []
    for p in range(2):
        first += [image_move(0, p, "z+"), image_move(0, 3 - p, "z-")]
    for q in range(2):
        first += [text_move(0, 0, 0, w, q) for w in ("x+", "x-")]
        first += [text_move(0, 0, 1, w, q) for w in ("y+", "y-")]
    for p in range(2):
        first += [image_move(0, 2 + p, "z+"), image_move(0, 1 - p, "z-")]
    for q in range(2):
        first += [text_move(0, 0, 0, "x2", q), text_move(0, 0, 1, "y2", q)]
    for q in range(2):
        first += [text_move(0, 0, 0, w, q) for w in ("y+", "y-")]
        first += [text_move(0, 0, 1, w, q) for w in ("x+", "x-")]
    first += [(("J", 0), "c", IR, 0, 64, 64)]
    forward("first", [], first)
    for p in range(4):
        for dz in (7, 6, 5):
            if dz != 5 or p < 2:
                forward(("fI", dz, p), [("I", dz, p)], [image_move(dz, p, "z+")])
        for dz in (1, 2, 3):
            if dz != 3 or p >= 2:
                forward(("fI", dz, p), [("I", dz, p)], [image_move(dz, p, "z-")])
    for dz in range(1, 8):
        forward(
            ("fJ", dz), [("I", dz, p) for p in range(4)],
            [(("J", dz), "c", IR, dz * 128, dz * 128 + 64, 64)],
        )
    text_parts = {}
    for half in range(2):
        two = "y" if half == 0 else "x"

        def at(a, b, half=half):
            return (a, b) if half == 0 else (b, a)

        def mv(a, b, way, q, half=half, at=at):
            return text_move(*at(a, b), half, way, q)

        for a in range(4):
            for q in range(2):
                here = ("T", *at(a, 0), half, q)
                if a != 0:
                    forward(
                        ("f1", half, a, q), [here], [mv(a, 0, two + "+", q), mv(a, 0, two + "-", q)]
                    )
                b, way = ((3, "+"), (1, "-"))[q]
                forward(
                    ("f2", half, a, b), [("T", *at(a, b), half, q)], [mv(a, b, two + way, q)]
                )
            for b in range(4):
                names = [("T", *at(a, b), half, q) for q in range(2)]
                text_parts[(*at(a, b), half)] = names if (a, b) != (0, 0) else []
    image_parts = {dz: [*(("I", dz, p) for p in range(4)), ("J", dz)] for dz in range(8)}
    image_parts[0] = [("J", 0)]

    def coef_block(r0, c0):
        acc = lax.dot_general(
            IR[r0 : r0 + 256, :], TR[c0 : c0 + 256, :], NT, preferred_element_type=F32
        )
        e = jnp.exp2(acc * (scale * LOG2E) + offset * LOG2E)
        d = 1.0 + e
        r = pltpu.reciprocal(d, approx=True)
        r = r * (2.0 - d * r)
        CF[r0 : r0 + 256, c0 : c0 + 256] = ((e * scale) * r).astype(BF16)
        q = e[:, :128] * d[:, 128:] + e[:, 128:]
        q = q[:128] * (1.0 + q[128:]) + q[128:]
        u = 1.0 + q
        term = jnp.log(u) + (q - (u - 1.0)) * pltpu.reciprocal(u, approx=True)
        LS[...] += jnp.sum(term.reshape(16, 8, 128), axis=0)

    def diagonal(group):
        for other in range(4):
            pair = c * 4 + other
            dz = lax.rem(pair - z + 8, 8)
            core = lax.rem(z + c, 2)
            key = lax.rem(other - x + 4, 4) * 4 + lax.rem(x - y + 4, 4)
            slot = sum(jnp.where(key == i, PLACE[i // 4, i % 4], 0) for i in range(16))

            @pl.when(jnp.logical_and(y == z // 2, slot // 4 == group))
            def _(dz=dz, core=core, slot=slot):
                r0 = pl.multiple_of(dz * 128 + core * 64, 64)
                c0 = pl.multiple_of((slot // 2) * 128, 128)
                shift = lax.rem(slot, 2) * 64
                acc = lax.dot_general(
                    IR[pl.ds(r0, 64), :], TR[pl.ds(c0, 128), :], NT, preferred_element_type=F32
                )
                logit = acc * scale + offset
                rows = lax.broadcasted_iota(jnp.int32, (64, 128), 0)
                cols = lax.broadcasted_iota(jnp.int32, (64, 128), 1)
                same = cols == rows + shift
                e = jnp.exp(logit)
                mine = (-scale / (1.0 + e)).astype(BF16)
                block = CF[pl.ds(r0, 64), pl.ds(c0, 128)]
                CF[pl.ds(r0, 64), pl.ds(c0, 128)] = jnp.where(
                    same, mine.astype(F32), block.astype(F32)
                ).astype(BF16)
                less = jnp.where(same, logit, 0.0)
                LS[...] -= jnp.sum(less.reshape(8, 8, 128), axis=0)

    for pair in (0, 3, 1, 2):
        for group in (3, 2, 1, 0):
            deps = image_parts[2 * pair] + image_parts[2 * pair + 1]
            for dx, dy in CHUNKS[4 * group : 4 * group + 4]:
                deps = deps + text_parts[dx, dy, 0] + text_parts[dx, dy, 1]
            plan.task(
                ("coef", pair, group), ["first", *deps], 0.32,
                functools.partial(coef_block, pair * 256, group * 256),
            )
    for group in range(4):
        plan.task(
            ("diag", group), [("coef", pair, group) for pair in range(4)], 0.1,
            functools.partial(diagonal, group),
        )
    diagonals = [("diag", group) for group in range(4)]

    def spread(name, dep, value, box, place, links, events):
        def run():
            box[pl.ds(place, 1)] = value().reshape(1, 8, 128)
            for link, event in zip(links, events):
                start(event, link, box.at[pl.ds(place, 1)], box.at[pl.ds(place, 1)])

        for link, event in zip(links, events):
            plan.send(event, "tiny", 0)
        plan.task(name, dep, 0.1, run, events)

    spread("loss0", diagonals, lambda: LS[...], LC, c, ["c"], [("Lc", 1)])
    dep = [("Lc", 1)]
    for name, box, before, place, span in (("x", LX, LC, x, 4), ("y", LY, LX, y, 4), ("z", LZ, LY, z, 8)):
        links = [(name, k) for k in range(1, span)]
        events = [("L" + name, k) for k in range(1, span)]
        spread("loss" + name, dep, functools.partial(lambda b: jnp.sum(b[...], axis=0), before), box, place, links, events)
        dep = events

    def loss_end():
        loss_ref[0] = jnp.sum(jnp.sum(LZ[...], axis=0)) * (1.0 / TOTAL)

    plan.task("loss", dep, 0.1, loss_end)

    def image_group(pair):
        part = jnp.dot(
            CF[pair * 256 : pair * 256 + 256, :], TR[...], preferred_element_type=F32
        )
        for k in range(2):
            dz = 2 * pair + k
            QI[dz * 64 : dz * 64 + 64, :] = part[k * 128 : k * 128 + 64]
            OI[dz * 64 : dz * 64 + 64, :] = part[k * 128 + 64 : k * 128 + 128]
            rows = pl.ds(dz * 64, 64)
            start(("D", dz), "c", OI.at[rows], DI.at[rows])

    def text_group(group):
        cols = slice(group * 256, group * 256 + 256)
        TP[cols, :] = lax.dot_general(CF[:, cols], IR[...], TN, preferred_element_type=F32)

    for dz in range(8):
        plan.send(("D", dz), "c", 128)
    for pair, group in ((2, 0), (1, 1), (3, 2), (0, 3)):
        plan.task(("TG", group), [("diag", group)], 0.9, functools.partial(text_group, group))
        plan.task(
            ("G", pair), diagonals, 0.9, functools.partial(image_group, pair),
            [("D", 2 * pair), ("D", 2 * pair + 1)],
        )

    zplace = {}

    def zbox(box, way, dz, p):
        i = zplace.setdefault((way, dz, p), len(zplace))
        return box.at[pl.ds(i * 16, 16)]

    def image_step(way, dz, p, arrived):
        rows = slice(dz * 64 + p * 16, dz * 64 + p * 16 + 16)
        v = QI[rows, :] + DI[rows, :]
        if arrived:
            before = dz + 1 if way == "z+" else dz - 1
            v = v + decode(zbox(ZR, way, before, p)[...])
        zbox(ZS, way, dz, p)[...] = encode(v)
        start(("R", way, dz, p), way, zbox(ZS, way, dz, p), zbox(ZR, way, dz, p))

    for way, places, long in (("z+", (4, 3, 2, 1), (0, 1)), ("z-", (4, 5, 6, 7), (2, 3))):
        for step, dz in enumerate(places):
            for p in range(4):
                if step == 0 and p not in long:
                    continue
                arrived = step > 1 or (step == 1 and p in long)
                deps = [("G", dz // 2), ("D", dz)]
                if arrived:
                    deps.append(("R", way, places[step - 1], p))
                event = plan.send(("R", way, dz, p), way, 16)
                plan.task(
                    ("step", way, dz, p), deps, 0.08,
                    functools.partial(image_step, way, dz, p, arrived), [event],
                )

    def project(emb_ref, rows, dgrad, out_ref):
        wide = emb_ref[rows, :].astype(F32)
        norm = jnp.sqrt(jnp.sum(wide * wide, axis=1, keepdims=True) + 1e-06)
        direction = wide / norm
        along = jnp.sum(direction * dgrad, axis=1, keepdims=True)
        out_ref[rows, :] = (dgrad - direction * along) / norm

    def image_end(p):
        rows = slice(p * 16, p * 16 + 16)
        v = QI[rows, :] + DI[rows, :]
        v = v + decode(zbox(ZR, "z+", 1, p)[...]) + decode(zbox(ZR, "z-", 7, p)[...])
        project(img_ref, rows, v, igrad_ref)

    for p in range(4):
        plan.task(
            ("image_end", p), [("G", 0), ("D", 0), ("R", "z+", 1, p), ("R", "z-", 7, p)], 0.15,
            functools.partial(image_end, p),
        )

    place = {}

    def ybox(box, key, rows):
        if key not in place:
            place[key] = sum(r for _, r in place.values()), rows
        return box.at[pl.ds(place[key][0], rows)]

    def put(event, way, v, rows):
        ybox(YS, event, rows)[...] = encode(v)
        start(event, way, ybox(YS, event, rows), ybox(YR, event, rows))

    def take(event, rows):
        return decode(ybox(YR, event, rows)[...])

    for half in range(2):
        one, two = ("y", "x") if half == 0 else ("x", "y")

        def rows_of(a, b, q=None, half=half):
            s = tslot(b, a, half) if half == 0 else tslot(a, b, half)
            if q is None:
                return slice(s, s + 32)
            return slice(s + 16 * q, s + 16 * q + 16)

        def group(a, b, half=half):
            return ("TG", PLACE[(b, a) if half == 0 else (a, b)] // 4)

        def step(b, a, q, arrived, event, way, half=half, rows_of=rows_of):
            v = TP[rows_of(a, b, q), :]
            if arrived:
                v = v + take(("U", half, b, 2, q), 16)
            put(event, way, v, 16)

        def joined(b, half=half, rows_of=rows_of):
            parts = []
            for q in range(2):
                v = TP[rows_of(0, b, q), :]
                parts.append(v + take(("U", half, b, 1, q), 16) + take(("U", half, b, 3, q), 16))
            return jnp.concatenate(parts, axis=0)

        def second(b, way, half=half, joined=joined):
            put(("V", half, b), way, joined(b), 32)

        def end(half=half, joined=joined):
            v = joined(0)
            for b in (1, 2, 3):
                v = v + take(("V", half, b), 32)
            project(txt_ref, slice(half * 32, half * 32 + 32), v, tgrad_ref)

        def add(b, a, q, way, arrived, half=half, step=step, group=group):
            event = plan.send(("U", half, b, a, q), way, 16)
            deps = [group(a, b)]
            if arrived:
                deps.append(("U", half, b, 2, q))
            plan.task(
                ("step", half, b, a, q), deps, 0.08,
                functools.partial(step, b, a, q, arrived, event, way), [event],
            )

        for b in (2, 1, 3, 0):
            add(b, 2, 0, one + "+", False)
            add(b, 2, 1, one + "-", False)
            for q in range(2):
                add(b, 1, q, one + "+", q == 0)
                add(b, 3, q, one + "-", q == 1)
            base = [group(0, b), *(("U", half, b, a, q) for a in (1, 3) for q in range(2))]
            if b != 0:
                way = two + {2: "2", 1: "+", 3: "-"}[b]
                event = plan.send(("V", half, b), way, 32)
                plan.task(
                    ("second", half, b), base, 0.15, functools.partial(second, b, way), [event]
                )
            else:
                plan.task(("text_end", half), [*base, *(("V", half, k) for k in (1, 2, 3))], 0.3, end)

    landed = set()

    def land(event):
        if event in plan.sends and event not in landed:
            copies[event].wait_recv()
            landed.add(event)

    for name, deps, fn, _ in plan.order():
        for event in deps:
            land(event)
        fn()
    for event in copies:
        land(event)
    for copy in copies.values():
        copy.wait_send()


def per_device(image_emb, text_emb, log_scale, bias):
    width = image_emb.shape[1]
    vmem = pl.BlockSpec(memory_space=pltpu.VMEM)
    hbm = pl.BlockSpec(memory_space=pltpu.HBM)
    smem = pl.BlockSpec(memory_space=pltpu.SMEM)
    ring = 28 * 16
    return pl.pallas_call(
        kernel,
        out_shape=(
            jax.ShapeDtypeStruct((1,), F32),
            jax.ShapeDtypeStruct((64, width), F32),
            jax.ShapeDtypeStruct((64, width), F32),
        ),
        in_specs=[hbm, hbm, smem, smem],
        out_specs=(smem, vmem, vmem),
        scratch_shapes=[
            pltpu.VMEM((1024, width), BF16),
            pltpu.VMEM((1024, width), BF16),
            pltpu.VMEM((1024, 1024), BF16),
            pltpu.VMEM((512, width), F32),
            pltpu.VMEM((512, width), F32),
            pltpu.VMEM((512, width), F32),
            pltpu.VMEM((1024, width), F32),
            pltpu.VMEM((ring, width), BF16),
            pltpu.VMEM((ring, width), BF16),
            pltpu.VMEM((960, width), BF16),
            pltpu.VMEM((960, width), BF16),
            pltpu.VMEM((8, 128), F32),
            pltpu.VMEM((2, 8, 128), F32),
            pltpu.VMEM((4, 8, 128), F32),
            pltpu.VMEM((4, 8, 128), F32),
            pltpu.VMEM((8, 8, 128), F32),
            pltpu.VMEM((64, width), BF16),
            pltpu.VMEM((64, width), BF16),
            pltpu.SemaphoreType.DMA((208,)),
            pltpu.SemaphoreType.DMA((208,)),
            pltpu.SemaphoreType.DMA((2,)),
        ],
        compiler_params=pltpu.CompilerParams(
            collective_id=0, has_side_effects=True, vmem_limit_bytes=30 << 20
        ),
        cost_estimate=pl.CostEstimate(
            flops=6 * 1024 * 1024 * width, bytes_accessed=64 * width * 12, transcendentals=1 << 22
        ),
    )(image_emb, text_emb, log_scale, bias)


def solution(mesh):
    in_specs = (P(("img", "txt"), None), P(("txt", "img"), None), P(), P())
    out_specs = (P(), P(("img", "txt"), None), P(("txt", "img"), None))
    return jax.shard_map(
        per_device, mesh=mesh, in_specs=in_specs, out_specs=out_specs, check_vma=False
    )
```

```python
import functools

import jax
import jax.numpy as jnp
from jax import lax
from jax.experimental import pallas as pl
from jax.experimental.pallas import tpu as pltpu
from jax.sharding import PartitionSpec as P

F32 = jnp.float32
BF16 = jnp.bfloat16
MESH = pl.DeviceIdType.MESH
NT = (((1,), (1,)), ((), ()))
TN = (((0,), (0,)), ((), ()))
TOTAL = 16384
LOG2E = 1.4426950408889634

CHUNKS = (
    (2, 2), (2, 1), (2, 3), (1, 2),
    (3, 2), (2, 0), (0, 2), (1, 1),
    (1, 3), (3, 1), (3, 3), (1, 0),
    (3, 0), (0, 1), (0, 3), (0, 0),
)
PLACE = {chunk: i for i, chunk in enumerate(CHUNKS)}
POWER = 7
RECEIVED = 131

ROW_US = 0.049
HOP_US = 3.0
FAR_US = 3.4
CORE_ROW_US = 0.005
CORE_HOP_US = 1.0


def encode(v):
    v2 = v * v
    return (v2 * v2 * v2 * v).astype(BF16)


def decode(w):
    w = w.astype(F32)
    m = jnp.exp2(jnp.log2(jnp.abs(w)) * (1.0 / POWER))
    return jnp.where(w < 0.0, -m, m)


class Plan:
    def __init__(self):
        self.tasks = []
        self.sends = {}
        self.group = {}

    def together(self, *events):
        for event in events:
            self.group[event] = events

    def send(self, event, link, rows):
        if link == "c":
            self.sends[event] = (("c",), rows * CORE_ROW_US, CORE_HOP_US)
        elif link == "tiny":
            self.sends[event] = ((), 0.0, 4.0)
        elif link[1] == "2":
            self.sends[event] = ((link[0] + "+", link[0] + "-"), rows * ROW_US, FAR_US)
        else:
            self.sends[event] = ((link,), rows * ROW_US, HOP_US)
        return event

    def task(self, name, deps, cost, fn, sends=()):
        wide = dict.fromkeys(e for d in deps for e in self.group.get(d, (d,)))
        self.tasks.append((name, tuple(wide), cost, fn, tuple(sends)))

    def levels(self):
        users, maker = {}, {}
        for i, (name, deps, _, _, sends) in enumerate(self.tasks):
            maker[name] = i
            for d in deps:
                users.setdefault(d, []).append(i)
        level = {}

        def of(i):
            if i not in level:
                name, _, cost, _, sends = self.tasks[i]
                after = [of(j) for j in users.get(name, ())]
                for e in sends:
                    _, wire, hop = self.sends[e]
                    after += [wire + hop + of(j) for j in users.get(e, ())]
                level[i] = cost + max(after, default=0.0)
            return level[i]

        return [of(i) for i in range(len(self.tasks))]

    def order(self):
        level = self.levels()
        done, free, out = {}, {}, []
        left = list(range(len(self.tasks)))
        now = 0.0
        while left:
            best = None
            for i in left:
                deps = self.tasks[i][1]
                if any(d not in done for d in deps):
                    continue
                ready = max([done[d] for d in deps], default=0.0)
                key = (max(ready, now), -level[i], i)
                if best is None or key < best:
                    best = key
            start, _, i = best
            left.remove(i)
            name, deps, cost, fn, sends = self.tasks[i]
            now = start + cost
            done[name] = now
            for event in sends:
                links, wire, hop = self.sends[event]
                begin = max([now, *(free.get(link, 0.0) for link in links)])
                for link in links:
                    free[link] = begin + wire
                done[event] = begin + wire + hop
            out.append((name, deps, fn, start))
        self.span = now
        return out


def kernel(
    img_hbm, txt_hbm, scale_ref, bias_ref, loss_ref, igrad_ref, tgrad_ref,
    IR, TR, CF, QI, OI, DI, TP, ZS, ZR, YS, YR, LS, LC, LX, LY, LZ, img_ref, txt_ref,
    send_sem, recv_sem, in_sem,
):
    img, txt = lax.axis_index("img"), lax.axis_index("txt")
    x, z, y, c = img // 8, img % 8, txt // 2, txt % 2

    def device(dx=0, dy=0, dz=0, dc=0):
        return (
            lax.rem(x + dx + 4, 4) * 8 + lax.rem(z + dz + 8, 8),
            lax.rem(y + dy + 4, 4) * 2 + lax.rem(c + dc, 2),
        )

    ways = {
        "x+": device(dx=1), "x-": device(dx=-1), "y+": device(dy=1), "y-": device(dy=-1),
        "z+": device(dz=1), "z-": device(dz=-1), "c": device(dc=1),
        "x2": device(dx=2), "y2": device(dy=2),
    }
    far = {("x", k): device(dx=k) for k in range(1, 4)}
    far |= {("y", k): device(dy=k) for k in range(1, 4)}
    far |= {("z", k): device(dz=k) for k in range(1, 8)}

    barrier = pltpu.get_barrier_semaphore()
    greeted = list(ways.values())
    for peer in greeted:
        pl.semaphore_signal(barrier, inc=1, device_id=peer, device_id_type=MESH)
    inputs = [
        pltpu.make_async_copy(img_hbm, img_ref, in_sem.at[0]),
        pltpu.make_async_copy(txt_hbm, txt_ref, in_sem.at[1]),
    ]
    for copy in inputs:
        copy.start()

    scale = jnp.exp(jnp.full((1, 1), scale_ref[0], F32))
    offset = jnp.full((1, 1), bias_ref[0], F32)

    def unit(ref):
        wide = ref[...].astype(F32)
        norm = jnp.sqrt(jnp.sum(wide * wide, axis=1, keepdims=True) + 1e-06)
        return (wide / norm).astype(BF16)

    LS[...] = jnp.zeros_like(LS)
    inputs[0].wait()
    IR[0:64, :] = unit(img_ref)
    inputs[1].wait()
    TR[960:1024, :] = unit(txt_ref)
    pl.semaphore_wait(barrier, len(greeted))

    plan = Plan()
    copies, pending, boxes = {}, {}, {}

    def start(event, link, src, dst, sent):
        peer = ways[link] if isinstance(link, str) else far[link]
        key = plan.group.get(event, (event,))
        index = boxes.setdefault(key, len(boxes))
        out = pending.setdefault(sent, [len(pending), 0])
        out[1] += src.shape[0]
        copy = pltpu.make_async_remote_copy(
            src_ref=src, dst_ref=dst, send_sem=send_sem.at[out[0]], recv_sem=recv_sem.at[index],
            device_id=peer, device_id_type=MESH,
        )
        copy.start()
        copies[event] = copy, dst.shape[0]

    landed = set()

    def land(event):
        key = plan.group.get(event, (event,))
        if event not in plan.sends or key in landed:
            return
        landed.add(key)
        if len(key) == 1:
            copies[event][0].wait_recv()
            return
        rows = sum(copies[e][1] for e in key)
        ref = whole[event[0]].at[pl.ds(0, rows)]
        pltpu.make_async_copy(ref, ref, recv_sem.at[boxes[key]]).wait()

    whole = {"I": IR, "J": IR, "T": TR, "R": IR, "U": IR, "V": IR, "Lx": LZ, "Ly": LZ, "Lz": LZ}

    def forward(name, deps, moves):
        def run():
            for event, link, ref, here, there, rows in moves:
                start(event, link, ref.at[pl.ds(here, rows)], ref.at[pl.ds(there, rows)], "I" if ref is IR else "T")

        for event, link, _, _, _, rows in moves:
            plan.send(event, link, rows)
        plan.task(name, deps, 0.02 + 0.03 * len(moves), run, [m[0] for m in moves])

    def islot(dz, p):
        return dz * 128 + p * 16

    def image_move(dz, p, way):
        to = (dz - 1) % 8 if way == "z+" else (dz + 1) % 8
        return (("I", to, p), way, IR, islot(dz, p), islot(to, p), 16)

    def tslot(dx, dy, half, q=0):
        return PLACE[dx, dy] * 64 + half * 32 + q * 16

    def text_move(dx, dy, half, way, q):
        step = {"+": -1, "-": 1, "2": 2}[way[1]]
        ex = (dx + step) % 4 if way[0] == "x" else dx
        ey = (dy + step) % 4 if way[0] == "y" else dy
        event = ("T", ex, ey, half, q)
        return (event, way, TR, tslot(dx, dy, half, q), tslot(ex, ey, half, q), 16)

    plan.together(*(("I", 4, p) for p in range(4)))
    plan.together(("I", 5, 2), ("I", 5, 3))
    plan.together(("I", 3, 0), ("I", 3, 1))
    for dz in (0, 2, 6):
        plan.together(("J", dz), ("J", dz + 1))
    for half in range(2):
        for a in range(4):
            places = [(a, b) if half == 0 else (b, a) for b in range(4)]
            plan.together(("T", *places[2], half, 0), ("T", *places[2], half, 1))
            plan.together(("T", *places[1], half, 0), ("T", *places[3], half, 1))

    first = []
    for p in range(2):
        first += [image_move(0, p, "z+"), image_move(0, 3 - p, "z-")]
    for q in range(2):
        first += [text_move(0, 0, 0, w, q) for w in ("x+", "x-")]
        first += [text_move(0, 0, 1, w, q) for w in ("y+", "y-")]
    for p in range(2):
        first += [image_move(0, 2 + p, "z+"), image_move(0, 1 - p, "z-")]
    for q in range(2):
        first += [text_move(0, 0, 0, "x2", q), text_move(0, 0, 1, "y2", q)]
    for q in range(2):
        first += [text_move(0, 0, 0, w, q) for w in ("y+", "y-")]
        first += [text_move(0, 0, 1, w, q) for w in ("x+", "x-")]
    first += [(("J", 0), "c", IR, 0, 64, 64)]
    forward("first", [], first)
    for p in range(4):
        for dz in (7, 6, 5):
            if dz != 5 or p < 2:
                forward(("fI", dz, p), [("I", dz, p)], [image_move(dz, p, "z+")])
        for dz in (1, 2, 3):
            if dz != 3 or p >= 2:
                forward(("fI", dz, p), [("I", dz, p)], [image_move(dz, p, "z-")])
    for dz in range(1, 8):
        forward(
            ("fJ", dz), [("I", dz, p) for p in range(4)],
            [(("J", dz), "c", IR, dz * 128, dz * 128 + 64, 64)],
        )
    text_parts = {}
    for half in range(2):
        two = "y" if half == 0 else "x"

        def at(a, b, half=half):
            return (a, b) if half == 0 else (b, a)

        def mv(a, b, way, q, half=half, at=at):
            return text_move(*at(a, b), half, way, q)

        for a in range(4):
            for q in range(2):
                here = ("T", *at(a, 0), half, q)
                if a != 0:
                    forward(
                        ("f1", half, a, q), [here], [mv(a, 0, two + "+", q), mv(a, 0, two + "-", q)]
                    )
                b, way = ((3, "+"), (1, "-"))[q]
                forward(
                    ("f2", half, a, b), [("T", *at(a, b), half, q)], [mv(a, b, two + way, q)]
                )
            for b in range(4):
                names = [("T", *at(a, b), half, q) for q in range(2)]
                text_parts[(*at(a, b), half)] = names if (a, b) != (0, 0) else []
    image_parts = {dz: [*(("I", dz, p) for p in range(4)), ("J", dz)] for dz in range(8)}
    image_parts[0] = [("J", 0)]

    def coef_block(r0, rows, c0, cols):
        acc = lax.dot_general(
            IR[r0 : r0 + rows, :], TR[c0 : c0 + cols, :], NT, preferred_element_type=F32
        )
        e = jnp.exp2(acc * (scale * LOG2E) + offset * LOG2E)
        d = 1.0 + e
        r = pltpu.reciprocal(d, approx=True)
        r = r * (2.0 - d * r)
        CF[r0 : r0 + rows, c0 : c0 + cols] = ((e * scale) * r).astype(BF16)
        w, h = cols // 2, rows // 2
        q = e[:, :w] * d[:, w:] + e[:, w:]
        q = q[:h] * (1.0 + q[h:]) + q[h:]
        u = 1.0 + q
        term = jnp.log(u) + (q - (u - 1.0)) * pltpu.reciprocal(u, approx=True)
        term = jnp.sum(term.reshape(h // 8, 8, w), axis=0)
        LS[...] += sum(term[:, k : k + 128] for k in range(0, w, 128))

    def diagonal(part):
        for other in range(4):
            pair = c * 4 + other
            dz = lax.rem(pair - z + 8, 8)
            core = lax.rem(z + c, 2)
            key = lax.rem(other - x + 4, 4) * 4 + lax.rem(x - y + 4, 4)
            slot = sum(jnp.where(key == i, PLACE[i // 4, i % 4], 0) for i in range(16))

            @pl.when(jnp.logical_and(y == z // 2, dz // 2 == part))
            def _(dz=dz, core=core, slot=slot):
                r0 = pl.multiple_of(dz * 128 + core * 64, 64)
                c0 = pl.multiple_of((slot // 2) * 128, 128)
                shift = lax.rem(slot, 2) * 64
                acc = lax.dot_general(
                    IR[pl.ds(r0, 64), :], TR[pl.ds(c0, 128), :], NT, preferred_element_type=F32
                )
                logit = acc * scale + offset
                rows = lax.broadcasted_iota(jnp.int32, (64, 128), 0)
                cols = lax.broadcasted_iota(jnp.int32, (64, 128), 1)
                same = cols == rows + shift
                e = jnp.exp(logit)
                mine = (-scale / (1.0 + e)).astype(BF16)
                block = CF[pl.ds(r0, 64), pl.ds(c0, 128)]
                CF[pl.ds(r0, 64), pl.ds(c0, 128)] = jnp.where(
                    same, mine.astype(F32), block.astype(F32)
                ).astype(BF16)
                less = jnp.where(same, logit, 0.0)
                LS[...] -= jnp.sum(less.reshape(8, 8, 128), axis=0)

    def text_ready(groups):
        deps = ["first"]
        for dx, dy in CHUNKS[4 * groups[0] : 4 * groups[-1] + 4]:
            deps += text_parts[dx, dy, 0] + text_parts[dx, dy, 1]
        return deps

    for pair in (0, 3, 1):
        for group in (3, 2, 1, 0):
            plan.task(
                ("coef", pair, group),
                image_parts[2 * pair] + image_parts[2 * pair + 1] + text_ready((group,)), 0.32,
                functools.partial(coef_block, pair * 256, 256, group * 256, 256),
            )
        plan.task(
            ("diag", pair), [("coef", pair, group) for group in range(4)], 0.1,
            functools.partial(diagonal, pair),
        )
    for dz in (5, 4):
        for groups in ((2, 3), (0, 1)):
            plan.task(
                ("coef", dz, groups), image_parts[dz] + text_ready(groups), 0.32,
                functools.partial(coef_block, dz * 128, 128, groups[0] * 256, 512),
            )
    plan.task(
        ("diag", 2), [("coef", dz, groups) for dz in (5, 4) for groups in ((2, 3), (0, 1))], 0.1,
        functools.partial(diagonal, 2),
    )
    diagonals = [("diag", pair) for pair in range(4)]

    def spread(name, dep, value, box, place, links, events):
        def run():
            box[pl.ds(place, 1)] = value().reshape(1, 8, 128)
            for link, event in zip(links, events):
                start(event, link, box.at[pl.ds(place, 1)], box.at[pl.ds(place, 1)], name)

        plan.together(*events)
        for link, event in zip(links, events):
            plan.send(event, "tiny", 0)
        plan.task(name, dep, 0.1, run, events)

    spread("loss0", diagonals, lambda: LS[...], LC, c, ["c"], [("Lc", 1)])
    dep = [("Lc", 1)]
    for name, box, before, place, span in (("x", LX, LC, x, 4), ("y", LY, LX, y, 4), ("z", LZ, LY, z, 8)):
        links = [(name, k) for k in range(1, span)]
        events = [("L" + name, k) for k in range(1, span)]
        spread("loss" + name, dep, functools.partial(lambda b: jnp.sum(b[...], axis=0), before), box, place, links, events)
        dep = events

    def loss_end():
        loss_ref[0] = jnp.sum(jnp.sum(LZ[...], axis=0)) * (1.0 / TOTAL)

    plan.task("loss", dep, 0.1, loss_end)

    def image_group(pair):
        part = jnp.dot(
            CF[pair * 256 : pair * 256 + 256, :], TR[...], preferred_element_type=F32
        )
        for k in range(2):
            dz = 2 * pair + k
            QI[dz * 64 : dz * 64 + 64, :] = part[k * 128 : k * 128 + 64]
            OI[dz * 64 : dz * 64 + 64, :] = part[k * 128 + 64 : k * 128 + 128]
            rows = pl.ds(dz * 64, 64)
            start(("D", dz), "c", OI.at[rows], DI.at[rows], "D")

    def text_group(group):
        cols = slice(group * 256, group * 256 + 256)
        TP[cols, :] = lax.dot_general(CF[:, cols], IR[...], TN, preferred_element_type=F32)

    for dz in range(8):
        plan.send(("D", dz), "c", 128)
    for pair, group in ((2, 0), (1, 1), (3, 2), (0, 3)):
        plan.task(("TG", group), diagonals, 0.9, functools.partial(text_group, group))
        plan.task(
            ("G", pair), [("diag", pair)], 0.9, functools.partial(image_group, pair),
            [("D", 2 * pair), ("D", 2 * pair + 1)],
        )

    zplace = {}

    def zbox(box, way, dz, p):
        i = zplace.setdefault((way, dz, p), len(zplace))
        return box.at[pl.ds(i * 16, 16)]

    def image_step(way, dz, p, arrived):
        rows = slice(dz * 64 + p * 16, dz * 64 + p * 16 + 16)
        v = QI[rows, :] + DI[rows, :]
        if arrived:
            before = dz + 1 if way == "z+" else dz - 1
            v = v + decode(zbox(ZR, way, before, p)[...])
        zbox(ZS, way, dz, p)[...] = encode(v)
        start(("R", way, dz, p), way, zbox(ZS, way, dz, p), zbox(ZR, way, dz, p), "R")

    ends = [("R", way, dz, p) for way, dz in (("z+", 1), ("z-", 7)) for p in range(4)]
    plan.together(*ends)
    for way, places, long in (("z+", (4, 3, 2, 1), (0, 1)), ("z-", (4, 5, 6, 7), (2, 3))):
        for step, dz in enumerate(places):
            for p in range(4):
                if step == 0 and p not in long:
                    continue
                arrived = step > 1 or (step == 1 and p in long)
                deps = [("G", dz // 2), ("D", dz)]
                if arrived:
                    deps.append(("R", way, places[step - 1], p))
                event = plan.send(("R", way, dz, p), way, 16)
                plan.task(
                    ("step", way, dz, p), deps, 0.08,
                    functools.partial(image_step, way, dz, p, arrived), [event],
                )

    def project(emb_ref, rows, dgrad, out_ref):
        wide = emb_ref[rows, :].astype(F32)
        norm = jnp.sqrt(jnp.sum(wide * wide, axis=1, keepdims=True) + 1e-06)
        direction = wide / norm
        along = jnp.sum(direction * dgrad, axis=1, keepdims=True)
        out_ref[rows, :] = (dgrad - direction * along) / norm

    def image_end():
        for p in range(4):
            rows = slice(p * 16, p * 16 + 16)
            v = QI[rows, :] + DI[rows, :]
            v = v + decode(zbox(ZR, "z+", 1, p)[...]) + decode(zbox(ZR, "z-", 7, p)[...])
            project(img_ref, rows, v, igrad_ref)

    plan.task("image_end", [("G", 0), ("D", 0), *ends], 0.5, image_end)

    place = {}

    def ybox(box, key, rows):
        if key not in place:
            place[key] = sum(r for _, r in place.values()), rows
        return box.at[pl.ds(place[key][0], rows)]

    def put(event, way, v, rows):
        ybox(YS, event, rows)[...] = encode(v)
        start(event, way, ybox(YS, event, rows), ybox(YR, event, rows), "Y")

    def take(event, rows):
        return decode(ybox(YR, event, rows)[...])

    for half in range(2):
        one, two = ("y", "x") if half == 0 else ("x", "y")

        def rows_of(a, b, q=None, half=half):
            s = tslot(b, a, half) if half == 0 else tslot(a, b, half)
            if q is None:
                return slice(s, s + 32)
            return slice(s + 16 * q, s + 16 * q + 16)

        def group(a, b, half=half):
            return ("TG", PLACE[(b, a) if half == 0 else (a, b)] // 4)

        def step(b, a, q, arrived, event, way, half=half, rows_of=rows_of):
            v = TP[rows_of(a, b, q), :]
            if arrived:
                v = v + take(("U", half, b, 2, q), 16)
            put(event, way, v, 16)

        def joined(b, half=half, rows_of=rows_of):
            parts = []
            for q in range(2):
                v = TP[rows_of(0, b, q), :]
                parts.append(v + take(("U", half, b, 1, q), 16) + take(("U", half, b, 3, q), 16))
            return jnp.concatenate(parts, axis=0)

        def second(b, way, half=half, joined=joined):
            put(("V", half, b), way, joined(b), 32)

        def end(half=half, joined=joined):
            v = joined(0)
            for b in (1, 2, 3):
                v = v + take(("V", half, b), 32)
            project(txt_ref, slice(half * 32, half * 32 + 32), v, tgrad_ref)

        def add(b, a, q, way, arrived, half=half, step=step, group=group):
            event = plan.send(("U", half, b, a, q), way, 16)
            deps = [group(a, b)]
            if arrived:
                deps.append(("U", half, b, 2, q))
            plan.task(
                ("step", half, b, a, q), deps, 0.08,
                functools.partial(step, b, a, q, arrived, event, way), [event],
            )

        plan.together(*(("V", half, b) for b in (1, 2, 3)))
        for b in (2, 1, 3, 0):
            plan.together(*(("U", half, b, a, q) for a in (1, 3) for q in range(2)))
            add(b, 2, 0, one + "+", False)
            add(b, 2, 1, one + "-", False)
            for q in range(2):
                add(b, 1, q, one + "+", q == 0)
                add(b, 3, q, one + "-", q == 1)
            base = [group(0, b), *(("U", half, b, a, q) for a in (1, 3) for q in range(2))]
            if b != 0:
                way = two + {2: "2", 1: "+", 3: "-"}[b]
                event = plan.send(("V", half, b), way, 32)
                plan.task(
                    ("second", half, b), base, 0.15, functools.partial(second, b, way), [event]
                )
            else:
                plan.task(("text_end", half), [*base, *(("V", half, k) for k in (1, 2, 3))], 0.3, end)

    for name, deps, fn, _ in plan.order():
        for event in deps:
            land(event)
        fn()
    for event in copies:
        land(event)
    sources = {"I": IR, "T": TR, "D": OI, "R": ZS, "Y": YS}
    for sent, (index, rows) in pending.items():
        ref = sources.get(sent, LZ).at[pl.ds(0, rows)]
        pltpu.make_async_copy(ref, ref, send_sem.at[index]).wait()


def per_device(image_emb, text_emb, log_scale, bias):
    width = image_emb.shape[1]
    vmem = pl.BlockSpec(memory_space=pltpu.VMEM)
    hbm = pl.BlockSpec(memory_space=pltpu.HBM)
    smem = pl.BlockSpec(memory_space=pltpu.SMEM)
    ring = 28 * 16
    return pl.pallas_call(
        kernel,
        out_shape=(
            jax.ShapeDtypeStruct((1,), F32),
            jax.ShapeDtypeStruct((64, width), F32),
            jax.ShapeDtypeStruct((64, width), F32),
        ),
        in_specs=[hbm, hbm, smem, smem],
        out_specs=(smem, vmem, vmem),
        scratch_shapes=[
            pltpu.VMEM((1024, width), BF16),
            pltpu.VMEM((1024, width), BF16),
            pltpu.VMEM((1024, 1024), BF16),
            pltpu.VMEM((512, width), F32),
            pltpu.VMEM((512, width), F32),
            pltpu.VMEM((512, width), F32),
            pltpu.VMEM((1024, width), F32),
            pltpu.VMEM((ring, width), BF16),
            pltpu.VMEM((ring, width), BF16),
            pltpu.VMEM((960, width), BF16),
            pltpu.VMEM((960, width), BF16),
            pltpu.VMEM((8, 128), F32),
            pltpu.VMEM((2, 8, 128), F32),
            pltpu.VMEM((4, 8, 128), F32),
            pltpu.VMEM((4, 8, 128), F32),
            pltpu.VMEM((8, 8, 128), F32),
            pltpu.VMEM((64, width), BF16),
            pltpu.VMEM((64, width), BF16),
            pltpu.SemaphoreType.DMA((9,)),
            pltpu.SemaphoreType.DMA((RECEIVED,)),
            pltpu.SemaphoreType.DMA((2,)),
        ],
        compiler_params=pltpu.CompilerParams(
            collective_id=0, has_side_effects=True, vmem_limit_bytes=30 << 20
        ),
        cost_estimate=pl.CostEstimate(
            flops=6 * 1024 * 1024 * width, bytes_accessed=64 * width * 12, transcendentals=1 << 22
        ),
    )(image_emb, text_emb, log_scale, bias)


def solution(mesh):
    in_specs = (P(("img", "txt"), None), P(("txt", "img"), None), P(), P())
    out_specs = (P(), P(("img", "txt"), None), P(("txt", "img"), None))
    return jax.shard_map(
        per_device, mesh=mesh, in_specs=in_specs, out_specs=out_specs, check_vma=False
    )
```

```python
import functools

import jax
import jax.numpy as jnp
from jax import lax
from jax.experimental import pallas as pl
from jax.experimental.pallas import tpu as pltpu
from jax.sharding import PartitionSpec as P

F32 = jnp.float32
BF16 = jnp.bfloat16
MESH = pl.DeviceIdType.MESH
NT = (((1,), (1,)), ((), ()))
TN = (((0,), (0,)), ((), ()))
TOTAL = 16384
LOG2E = 1.4426950408889634

CHUNKS = (
    (2, 2), (2, 1), (2, 3), (1, 2),
    (3, 2), (2, 0), (0, 2), (1, 1),
    (1, 3), (3, 1), (3, 3), (1, 0),
    (3, 0), (0, 1), (0, 3), (0, 0),
)
PLACE = {chunk: i for i, chunk in enumerate(CHUNKS)}
POWER = 7
RECEIVED = 93
DIRECT = (2,)

ROW_US = 0.049
HOP_US = 3.0
FAR_US = 3.4
CORE_ROW_US = 0.005
SLACK_US = 0.0
STEP_US = 0.12
COEF_US = 0.25
CORE_HOP_US = 1.0


def encode(v):
    v2 = v * v
    return (v2 * v2 * v2 * v).astype(BF16)


def decode(w):
    w = w.astype(F32)
    m = jnp.exp2(jnp.log2(jnp.abs(w)) * (1.0 / POWER))
    return jnp.where(w < 0.0, -m, m)


class Plan:
    def __init__(self):
        self.tasks = []
        self.sends = {}
        self.group = {}

    def together(self, *events):
        for event in events:
            self.group[event] = events

    def send(self, event, link, rows):
        if link == "c":
            self.sends[event] = (("c",), rows * CORE_ROW_US, CORE_HOP_US)
        elif link == "tiny":
            self.sends[event] = ((), 0.0, 4.0)
        elif link[1] == "2":
            self.sends[event] = ((link[0] + "+", link[0] + "-"), rows * ROW_US, FAR_US)
        else:
            self.sends[event] = ((link,), rows * ROW_US, HOP_US)
        return event

    def task(self, name, deps, cost, fn, sends=()):
        wide = dict.fromkeys(e for d in deps for e in self.group.get(d, (d,)))
        self.tasks.append((name, tuple(wide), cost, fn, tuple(sends)))

    def levels(self):
        users, maker = {}, {}
        for i, (name, deps, _, _, sends) in enumerate(self.tasks):
            maker[name] = i
            for d in deps:
                users.setdefault(d, []).append(i)
        level = {}

        def of(i):
            if i not in level:
                name, _, cost, _, sends = self.tasks[i]
                after = [of(j) for j in users.get(name, ())]
                for e in sends:
                    _, wire, hop = self.sends[e]
                    after += [wire + hop + of(j) for j in users.get(e, ())]
                level[i] = cost + max(after, default=0.0)
            return level[i]

        return [of(i) for i in range(len(self.tasks))]

    def order(self):
        level = self.levels()
        done, free, out = {}, {}, []
        left = list(range(len(self.tasks)))
        now = 0.0
        while left:
            best = None
            for i in left:
                deps = self.tasks[i][1]
                if any(d not in done for d in deps):
                    continue
                ready = max([done[d] for d in deps], default=0.0)
                slack = SLACK_US if self.tasks[i][2] > 0.24 else 0.0
                key = (max(ready + slack, now), -level[i], i)
                if best is None or key < best[0]:
                    best = key, ready
            (_, _, i), ready = best
            left.remove(i)
            name, deps, cost, fn, sends = self.tasks[i]
            start = max(ready, now)
            now = start + cost
            done[name] = now
            for event in sends:
                links, wire, hop = self.sends[event]
                begin = max([now, *(free.get(link, 0.0) for link in links)])
                for link in links:
                    free[link] = begin + wire
                done[event] = begin + wire + hop
            out.append((name, deps, fn, start))
        self.span = now
        return out


def kernel(
    both_ref, scale_ref, bias_ref, loss_ref, igrad_ref, tgrad_ref,
    IR, TR, CF, QI, OI, DI, TP, ZS, ZR, YS, YR, LS, LC, LX, LY, LZ,
    send_sem, recv_sem,
):
    img, txt = lax.axis_index("img"), lax.axis_index("txt")
    x, z, y, c = img // 8, img % 8, txt // 2, txt % 2

    def device(dx=0, dy=0, dz=0, dc=0):
        return (
            lax.rem(x + dx + 4, 4) * 8 + lax.rem(z + dz + 8, 8),
            lax.rem(y + dy + 4, 4) * 2 + lax.rem(c + dc, 2),
        )

    ways = {
        "x+": device(dx=1), "x-": device(dx=-1), "y+": device(dy=1), "y-": device(dy=-1),
        "z+": device(dz=1), "z-": device(dz=-1), "c": device(dc=1),
        "x2": device(dx=2), "y2": device(dy=2),
    }
    far = {("x", k): device(dx=k) for k in range(1, 4)}
    far |= {("y", k): device(dy=k) for k in range(1, 4)}
    far |= {("z", k): device(dz=k) for k in range(1, 8)}

    barrier = pltpu.get_barrier_semaphore()
    greeted = list(ways.values())
    for peer in greeted:
        pl.semaphore_signal(barrier, inc=1, device_id=peer, device_id_type=MESH)
    img_ref, txt_ref = both_ref.at[pl.ds(0, 64)], both_ref.at[pl.ds(64, 64)]
    scale = jnp.exp(jnp.full((1, 1), scale_ref[0], F32))
    offset = jnp.full((1, 1), bias_ref[0], F32)

    def unit(ref):
        wide = ref[...].astype(F32)
        norm = jnp.sqrt(jnp.sum(wide * wide, axis=1, keepdims=True) + 1e-06)
        return (wide / norm).astype(BF16)

    LS[...] = jnp.zeros_like(LS)
    IR[0:64, :] = unit(img_ref)
    TR[960:1024, :] = unit(txt_ref)
    pl.semaphore_wait(barrier, len(greeted))

    plan = Plan()
    copies, pending, boxes = {}, {}, {}

    def start(event, link, src, dst, sent):
        peer = ways[link] if isinstance(link, str) else far[link]
        key = plan.group.get(event, (event,))
        index = boxes.setdefault(key, len(boxes))
        out = pending.setdefault(sent, [len(pending), 0])
        out[1] += src.shape[0]
        copy = pltpu.make_async_remote_copy(
            src_ref=src, dst_ref=dst, send_sem=send_sem.at[out[0]], recv_sem=recv_sem.at[index],
            device_id=peer, device_id_type=MESH,
        )
        copy.start()
        copies[event] = copy, dst.shape[0]

    landed = set()

    def land(event):
        key = plan.group.get(event, (event,))
        if event not in plan.sends or key in landed:
            return
        landed.add(key)
        if len(key) == 1:
            copies[event][0].wait_recv()
            return
        rows = sum(copies[e][1] for e in key)
        ref = whole[event[0]].at[pl.ds(0, rows)]
        pltpu.make_async_copy(ref, ref, recv_sem.at[boxes[key]]).wait()

    whole = {"I": IR, "J": IR, "T": TR, "R": IR, "U": IR, "V": IR, "Lx": LZ, "Ly": LZ, "Lz": LZ}

    def forward(name, deps, moves):
        def run():
            for event, link, ref, here, there, rows in moves:
                start(event, link, ref.at[pl.ds(here, rows)], ref.at[pl.ds(there, rows)], "I" if ref is IR else "T")

        for event, link, _, _, _, rows in moves:
            plan.send(event, link, rows)
        plan.task(name, deps, 0.02 + 0.03 * len(moves), run, [m[0] for m in moves])

    def islot(dz, p):
        return dz * 128 + p * 16

    def image_move(dz, p, way):
        to = (dz - 1) % 8 if way == "z+" else (dz + 1) % 8
        return (("I", to, p), way, IR, islot(dz, p), islot(to, p), 16)

    def tslot(dx, dy, half, q=0):
        return PLACE[dx, dy] * 64 + half * 32 + q * 16

    def text_move(dx, dy, half, way, q):
        step = {"+": -1, "-": 1, "2": 2}[way[1]]
        ex = (dx + step) % 4 if way[0] == "x" else dx
        ey = (dy + step) % 4 if way[0] == "y" else dy
        event = ("T", ex, ey, half, q)
        return (event, way, TR, tslot(dx, dy, half, q), tslot(ex, ey, half, q), 16)

    plan.together(("I", 4, 0), ("I", 4, 1))
    plan.together(("I", 4, 2), ("I", 4, 3))
    plan.together(("J", 4, 0), ("J", 4, 1))
    plan.together(("I", 5, 2), ("I", 5, 3))
    plan.together(("I", 3, 0), ("I", 3, 1))
    for dz in (0, 2, 6):
        plan.together(("J", dz), ("J", dz + 1))
    for half in range(2):
        for a in range(4):
            places = [(a, b) if half == 0 else (b, a) for b in range(4)]
            plan.together(("T", *places[2], half, 0), ("T", *places[2], half, 1))
            if a in DIRECT:
                plan.together(("T", *places[1], half, 0), ("T", *places[1], half, 1))
                plan.together(("T", *places[3], half, 0), ("T", *places[3], half, 1))
            else:
                plan.together(("T", *places[1], half, 0), ("T", *places[3], half, 1))

    first = []
    for p in range(2):
        first += [image_move(0, p, "z+"), image_move(0, 3 - p, "z-")]
    for q in range(2):
        first += [text_move(0, 0, 0, w, q) for w in ("x+", "x-")]
        first += [text_move(0, 0, 1, w, q) for w in ("y+", "y-")]
    for p in range(2):
        first += [image_move(0, 2 + p, "z+"), image_move(0, 1 - p, "z-")]
    for q in range(2):
        first += [text_move(0, 0, 0, "x2", q), text_move(0, 0, 1, "y2", q)]
    for q in range(2):
        first += [text_move(0, 0, 0, w, q) for w in ("y+", "y-")]
        first += [text_move(0, 0, 1, w, q) for w in ("x+", "x-")]
    first += [(("J", 0), "c", IR, 0, 64, 64)]
    forward("first", [], first)
    for step in range(1, 4):
        for p in range(4 if step < 3 else 2):
            here = [("I", 8 - step, p), ("I", step, 3 - p)]
            plan.together(*here)
            moves = [image_move(8 - step, p, "z+"), image_move(step, 3 - p, "z-")]
            forward(("fI", step, p), here, moves)
    for dz in (1, 2, 3, 5, 6, 7):
        forward(
            ("fJ", dz), [("I", dz, p) for p in range(4)],
            [(("J", dz), "c", IR, dz * 128, dz * 128 + 64, 64)],
        )
    for k in range(2):
        forward(
            ("fJ", 4, k), [("I", 4, 2 * k), ("I", 4, 2 * k + 1)],
            [(("J", 4, k), "c", IR, 512 + k * 32, 576 + k * 32, 32)],
        )
    text_parts = {}
    for half in range(2):
        two = "y" if half == 0 else "x"

        def at(a, b, half=half):
            return (a, b) if half == 0 else (b, a)

        def mv(a, b, way, q, half=half, at=at):
            return text_move(*at(a, b), half, way, q)

        for a in range(4):
            for q in range(2):
                here = ("T", *at(a, 0), half, q)
                if a != 0:
                    moves = [mv(a, 0, two + "+", q), mv(a, 0, two + "-", q)]
                    if a in DIRECT:
                        moves.append(mv(a, 0, two + "2", q))
                    forward(("f1", half, a, q), [here], moves)
                if a in DIRECT:
                    continue
                b, way = ((3, "+"), (1, "-"))[q]
                forward(
                    ("f2", half, a, b), [("T", *at(a, b), half, q)], [mv(a, b, two + way, q)]
                )
            for b in range(4):
                names = [("T", *at(a, b), half, q) for q in range(2)]
                text_parts[(*at(a, b), half)] = names if (a, b) != (0, 0) else []
    image_parts = {dz: [*(("I", dz, p) for p in range(4)), ("J", dz)] for dz in range(8)}
    image_parts[0] = [("J", 0)]
    image_parts[4][-1:] = [("J", 4, 0), ("J", 4, 1)]

    def coef_block(r0, rows, c0, cols):
        acc = lax.dot_general(
            IR[r0 : r0 + rows, :], TR[c0 : c0 + cols, :], NT, preferred_element_type=F32
        )
        e = jnp.exp2(acc * (scale * LOG2E) + offset * LOG2E)
        d = 1.0 + e
        r = pltpu.reciprocal(d, approx=True)
        r = r * (2.0 - d * r)
        CF[r0 : r0 + rows, c0 : c0 + cols] = ((e * scale) * r).astype(BF16)
        w, h = cols // 2, rows // 2
        q = e[:, :w] * d[:, w:] + e[:, w:]
        q = q[:h] * (1.0 + q[h:]) + q[h:]
        u = 1.0 + q
        term = jnp.log(u) + (q - (u - 1.0)) * pltpu.reciprocal(u, approx=True)
        term = jnp.sum(term.reshape(h // 8, 8, w), axis=0)
        LS[...] += sum(term[:, k : k + 128] for k in range(0, w, 128))

    def diagonal(part):
        for other in range(4):
            pair = c * 4 + other
            dz = lax.rem(pair - z + 8, 8)
            core = lax.rem(z + c, 2)
            key = lax.rem(other - x + 4, 4) * 4 + lax.rem(x - y + 4, 4)
            slot = sum(jnp.where(key == i, PLACE[i // 4, i % 4], 0) for i in range(16))

            @pl.when(jnp.logical_and(y == z // 2, dz // 2 == part))
            def _(dz=dz, core=core, slot=slot):
                r0 = pl.multiple_of(dz * 128 + core * 64, 64)
                t0 = pl.multiple_of(slot * 64, 64)
                c0 = pl.multiple_of((slot // 2) * 128, 128)
                shift = lax.rem(slot, 2) * 64
                pairs = IR[pl.ds(r0, 64), :].astype(F32) * TR[pl.ds(t0, 64), :].astype(F32)
                logit = jnp.sum(pairs, axis=1, keepdims=True) * scale + offset
                rows = lax.broadcasted_iota(jnp.int32, (64, 128), 0)
                cols = lax.broadcasted_iota(jnp.int32, (64, 128), 1)
                same = cols == rows + shift
                mine = -scale / (1.0 + jnp.exp(logit))
                block = CF[pl.ds(r0, 64), pl.ds(c0, 128)].astype(F32)
                CF[pl.ds(r0, 64), pl.ds(c0, 128)] = jnp.where(same, mine, block).astype(BF16)
                less = jnp.where(same, logit, 0.0)
                LS[...] -= jnp.sum(less.reshape(8, 8, 128), axis=0)

    def text_ready(groups):
        deps = ["first"]
        for dx, dy in CHUNKS[4 * groups[0] : 4 * groups[-1] + 4]:
            deps += text_parts[dx, dy, 0] + text_parts[dx, dy, 1]
        return deps

    for pair in (0, 3, 1, 2):
        for group in (3, 2, 1, 0):
            plan.task(
                ("coef", pair, group),
                image_parts[2 * pair] + image_parts[2 * pair + 1] + text_ready((group,)), COEF_US,
                functools.partial(coef_block, pair * 256, 256, group * 256, 256),
            )
        plan.task(
            ("diag", pair), [("coef", pair, group) for group in range(4)], 0.1,
            functools.partial(diagonal, pair),
        )
    diagonals = [("diag", pair) for pair in range(4)]

    def spread(name, dep, value, box, place, links, events):
        def run():
            box[pl.ds(place, 1)] = value().reshape(1, 8, 128)
            for link, event in zip(links, events):
                start(event, link, box.at[pl.ds(place, 1)], box.at[pl.ds(place, 1)], name)

        plan.together(*events)
        for link, event in zip(links, events):
            plan.send(event, "tiny", 0)
        plan.task(name, dep, 0.1, run, events)

    spread("loss0", diagonals, lambda: LS[...], LC, c, ["c"], [("Lc", 1)])
    dep = [("Lc", 1)]
    for name, box, before, place, span in (("x", LX, LC, x, 4), ("y", LY, LX, y, 4), ("z", LZ, LY, z, 8)):
        links = [(name, k) for k in range(1, span)]
        events = [("L" + name, k) for k in range(1, span)]
        spread("loss" + name, dep, functools.partial(lambda b: jnp.sum(b[...], axis=0), before), box, place, links, events)
        dep = events

    def loss_end():
        loss_ref[0] = jnp.sum(jnp.sum(LZ[...], axis=0)) * (1.0 / TOTAL)

    plan.task("loss", dep, 0.1, loss_end)

    def image_group(pair):
        part = jnp.dot(
            CF[pair * 256 : pair * 256 + 256, :], TR[...], preferred_element_type=F32
        )
        for k in range(2):
            dz = 2 * pair + k
            QI[dz * 64 : dz * 64 + 64, :] = part[k * 128 : k * 128 + 64]
            OI[dz * 64 : dz * 64 + 64, :] = part[k * 128 + 64 : k * 128 + 128]
            rows = pl.ds(dz * 64, 64)
            start(("D", dz), "c", OI.at[rows], DI.at[rows], "D")

    def text_group(group):
        cols = slice(group * 256, group * 256 + 256)
        TP[cols, :] = lax.dot_general(CF[:, cols], IR[...], TN, preferred_element_type=F32)

    for dz in range(8):
        plan.send(("D", dz), "c", 128)
    for pair, group in ((2, 0), (1, 1), (3, 2), (0, 3)):
        plan.task(("TG", group), diagonals, 0.8, functools.partial(text_group, group))
        plan.task(
            ("G", pair), [("diag", pair)], 0.8, functools.partial(image_group, pair),
            [("D", 2 * pair), ("D", 2 * pair + 1)],
        )

    zplace = {}

    def zbox(box, way, dz, p):
        i = zplace.setdefault((way, dz, p), len(zplace))
        return box.at[pl.ds(i * 16, 16)]

    def run_all(parts):
        for work, _ in parts:
            work()
        for _, go in parts:
            go()

    def image_part(way, dz, p, arrived):
        def work():
            rows = slice(dz * 64 + p * 16, dz * 64 + p * 16 + 16)
            v = QI[rows, :] + DI[rows, :]
            if arrived:
                before = dz + 1 if way == "z+" else dz - 1
                v = v + decode(zbox(ZR, way, before, p)[...])
            zbox(ZS, way, dz, p)[...] = encode(v)

        def go():
            start(("R", way, dz, p), way, zbox(ZS, way, dz, p), zbox(ZR, way, dz, p), "R")

        return work, go

    ends = [("R", way, dz, p) for way, dz in (("z+", 1), ("z-", 7)) for p in range(4)]
    plan.together(*ends)
    for step in range(4):
        for p in range(4):
            if step == 0 and p > 1:
                continue
            arrived = step > 1 or (step == 1 and p < 2)
            near, away = ("z+", 4 - step, p), ("z-", 4 + step, 3 - p)
            deps = [("G", near[1] // 2), ("D", near[1]), ("G", away[1] // 2), ("D", away[1])]
            if arrived:
                deps += [("R", "z+", 5 - step, p), ("R", "z-", 3 + step, 3 - p)]
            events = [plan.send(("R", *near), "z+", 16), plan.send(("R", *away), "z-", 16)]
            if step < 3:
                plan.together(*events)
            parts = [image_part(*near, arrived), image_part(*away, arrived)]
            plan.task(("step", step, p), deps, STEP_US, functools.partial(run_all, parts), events)

    def project(emb_ref, rows, dgrad, out_ref):
        wide = emb_ref[rows, :].astype(F32)
        norm = jnp.sqrt(jnp.sum(wide * wide, axis=1, keepdims=True) + 1e-06)
        direction = wide / norm
        along = jnp.sum(direction * dgrad, axis=1, keepdims=True)
        out_ref[rows, :] = (dgrad - direction * along) / norm

    def image_end():
        for p in range(4):
            rows = slice(p * 16, p * 16 + 16)
            v = QI[rows, :] + DI[rows, :]
            v = v + decode(zbox(ZR, "z+", 1, p)[...]) + decode(zbox(ZR, "z-", 7, p)[...])
            project(img_ref, rows, v, igrad_ref)

    plan.task("image_end", [("G", 0), ("D", 0), *ends], 0.5, image_end)

    place = {}

    def ybox(box, key, rows):
        if key not in place:
            place[key] = sum(r for _, r in place.values()), rows
        return box.at[pl.ds(place[key][0], rows)]

    def take(event, rows):
        return decode(ybox(YR, event, rows)[...])

    def rows_of(half, a, b, q=None):
        start_row = tslot(b, a, half) if half == 0 else tslot(a, b, half)
        if q is None:
            return slice(start_row, start_row + 32)
        return slice(start_row + 16 * q, start_row + 16 * q + 16)

    def group(half, a, b):
        return ("TG", PLACE[(b, a) if half == 0 else (a, b)] // 4)

    def text_part(half, b, a, q, way, arrived):
        event = ("U", half, b, a, q)

        def work():
            v = TP[rows_of(half, a, b, q), :]
            if arrived:
                v = v + take(("U", half, b, 2, q), 16)
            ybox(YS, event, 16)[...] = encode(v)

        def go():
            start(event, way, ybox(YS, event, 16), ybox(YR, event, 16), "Y")

        return work, go

    def joined(half, b):
        parts = []
        for q in range(2):
            v = TP[rows_of(half, 0, b, q), :]
            for a in (1, 3):
                v = v + take(("U", half, b, a, q), 16)
            parts.append(v)
        return jnp.concatenate(parts, axis=0)

    def second_part(half, b, way):
        event = ("V", half, b)

        def work():
            ybox(YS, event, 32)[...] = encode(joined(half, b))

        def go():
            start(event, way, ybox(YS, event, 32), ybox(YR, event, 32), "Y")

        return work, go

    def text_end():
        for half in range(2):
            v = joined(half, 0)
            for b in (1, 2, 3):
                v = v + take(("V", half, b), 32)
            project(txt_ref, slice(half * 32, half * 32 + 32), v, tgrad_ref)

    one, two = ("y", "x"), ("x", "y")
    sides = ((1, "+"), (3, "-"))
    plan.together(*(("V", half, b) for half in range(2) for b in (1, 2, 3)))
    for b in (2, 1, 3, 0):
        outer, fresh, passed = [], [], []
        for half in range(2):
            for q, (a, sign) in enumerate(sides):
                outer.append((half, b, 2, q, one[half] + sign, False))
                fresh.append((half, b, a, 1 - q, one[half] + sign, False))
                passed.append((half, b, a, q, one[half] + sign, True))
        plan.together(*(("U", *part[:4]) for part in outer))
        plan.together(*(("U", *part[:4]) for part in fresh + passed))
        for kind, parts in (("outer", outer), ("fresh", fresh), ("passed", passed)):
            events = [plan.send(("U", *part[:4]), part[4], 16) for part in parts]
            deps = [group(part[0], part[2], b) for part in parts]
            if kind == "passed":
                deps += [("U", half, b, 2, q) for half in range(2) for q in range(2)]
            run = functools.partial(run_all, [text_part(*part) for part in parts])
            plan.task((kind, b), deps, 2 * STEP_US, run, events)
        base = [group(half, 0, b) for half in range(2)]
        base += [("U", *part[:4]) for part in fresh + passed]
        if b != 0:
            ways_two = [two[half] + {2: "2", 1: "+", 3: "-"}[b] for half in range(2)]
            events = [plan.send(("V", half, b), ways_two[half], 32) for half in range(2)]
            parts = [second_part(half, b, ways_two[half]) for half in range(2)]
            plan.task(("second", b), base, 0.25, functools.partial(run_all, parts), events)
        else:
            last = [("V", half, k) for half in range(2) for k in (1, 2, 3)]
            plan.task("text_end", [*base, *last], 0.5, text_end)

    for name, deps, fn, _ in plan.order():
        for event in deps:
            land(event)
        fn()
    for event in copies:
        land(event)
    sources = {"I": IR, "T": TR, "D": OI, "R": ZS, "Y": YS}
    assert len(boxes) == RECEIVED
    for sent, (index, rows) in pending.items():
        ref = sources.get(sent, LZ).at[pl.ds(0, rows)]
        pltpu.make_async_copy(ref, ref, send_sem.at[index]).wait()


def per_device(image_emb, text_emb, log_scale, bias):
    width = image_emb.shape[1]
    vmem = pl.BlockSpec(memory_space=pltpu.VMEM)
    smem = pl.BlockSpec(memory_space=pltpu.SMEM)
    ring = 28 * 16
    return pl.pallas_call(
        kernel,
        out_shape=(
            jax.ShapeDtypeStruct((1,), F32),
            jax.ShapeDtypeStruct((64, width), F32),
            jax.ShapeDtypeStruct((64, width), F32),
        ),
        in_specs=[vmem, smem, smem],
        out_specs=(smem, vmem, vmem),
        scratch_shapes=[
            pltpu.VMEM((1024, width), BF16),
            pltpu.VMEM((1024, width), BF16),
            pltpu.VMEM((1024, 1024), BF16),
            pltpu.VMEM((512, width), F32),
            pltpu.VMEM((512, width), F32),
            pltpu.VMEM((512, width), F32),
            pltpu.VMEM((1024, width), F32),
            pltpu.VMEM((ring, width), BF16),
            pltpu.VMEM((ring, width), BF16),
            pltpu.VMEM((960, width), BF16),
            pltpu.VMEM((960, width), BF16),
            pltpu.VMEM((8, 128), F32),
            pltpu.VMEM((2, 8, 128), F32),
            pltpu.VMEM((4, 8, 128), F32),
            pltpu.VMEM((4, 8, 128), F32),
            pltpu.VMEM((8, 8, 128), F32),
            pltpu.SemaphoreType.DMA((9,)),
            pltpu.SemaphoreType.DMA((RECEIVED,)),
        ],
        compiler_params=pltpu.CompilerParams(
            collective_id=0, has_side_effects=True, vmem_limit_bytes=30 << 20
        ),
        cost_estimate=pl.CostEstimate(
            flops=6 * 1024 * 1024 * width, bytes_accessed=64 * width * 12, transcendentals=1 << 22
        ),
    )(jnp.concatenate([image_emb, text_emb], axis=0), log_scale, bias)


def solution(mesh):
    in_specs = (P(("img", "txt"), None), P(("txt", "img"), None), P(), P())
    out_specs = (P(), P(("img", "txt"), None), P(("txt", "img"), None))
    return jax.shard_map(
        per_device, mesh=mesh, in_specs=in_specs, out_specs=out_specs, check_vma=False
    )
```

```python
import functools

import jax
import jax.numpy as jnp
from jax import lax
from jax.experimental import pallas as pl
from jax.experimental.pallas import tpu as pltpu
from jax.sharding import PartitionSpec as P

F32 = jnp.float32
BF16 = jnp.bfloat16
MESH = pl.DeviceIdType.MESH
NT = (((1,), (1,)), ((), ()))
TN = (((0,), (0,)), ((), ()))
TOTAL = 16384
LOG2E = 1.4426950408889634

CHUNKS = (
    (2, 2), (2, 1), (2, 3), (1, 2),
    (3, 2), (2, 0), (0, 2), (1, 1),
    (1, 3), (3, 1), (3, 3), (1, 0),
    (3, 0), (0, 1), (0, 3), (0, 0),
)
PLACE = {chunk: i for i, chunk in enumerate(CHUNKS)}
POWER = 7
RECEIVED = 95
DIRECT = ()

ROW_US = 0.049
HOP_US = 3.0
FAR_US = 3.4
CORE_ROW_US = 0.005
SLACK_US = 0.0
STEP_US = 0.2
COEF_US = 0.35
CORE_HOP_US = 1.0


def encode(v):
    v2 = v * v
    return (v2 * v2 * v2 * v).astype(BF16)


def decode(w):
    w = w.astype(F32)
    m = jnp.exp2(jnp.log2(jnp.abs(w)) * (1.0 / POWER))
    return jnp.where(w < 0.0, -m, m)


class Plan:
    def __init__(self):
        self.tasks = []
        self.sends = {}
        self.group = {}

    def together(self, *events):
        for event in events:
            self.group[event] = events

    def send(self, event, link, rows):
        if link == "c":
            self.sends[event] = (("c",), rows * CORE_ROW_US, CORE_HOP_US)
        elif link == "tiny":
            self.sends[event] = ((), 0.0, 4.0)
        elif link[1] == "2":
            self.sends[event] = ((link[0] + "+", link[0] + "-"), rows * ROW_US, FAR_US)
        else:
            self.sends[event] = ((link,), rows * ROW_US, HOP_US)
        return event

    def task(self, name, deps, cost, fn, sends=()):
        wide = dict.fromkeys(e for d in deps for e in self.group.get(d, (d,)))
        self.tasks.append((name, tuple(wide), cost, fn, tuple(sends)))

    def levels(self):
        users, maker = {}, {}
        for i, (name, deps, _, _, sends) in enumerate(self.tasks):
            maker[name] = i
            for d in deps:
                users.setdefault(d, []).append(i)
        level = {}

        def of(i):
            if i not in level:
                name, _, cost, _, sends = self.tasks[i]
                after = [of(j) for j in users.get(name, ())]
                for e in sends:
                    _, wire, hop = self.sends[e]
                    after += [wire + hop + of(j) for j in users.get(e, ())]
                level[i] = cost + max(after, default=0.0)
            return level[i]

        return [of(i) for i in range(len(self.tasks))]

    def order(self):
        level = self.levels()
        done, free, out = {}, {}, []
        left = list(range(len(self.tasks)))
        now = 0.0
        while left:
            best = None
            for i in left:
                deps = self.tasks[i][1]
                if any(d not in done for d in deps):
                    continue
                ready = max([done[d] for d in deps], default=0.0)
                slack = SLACK_US if self.tasks[i][2] > 0.24 else 0.0
                key = (max(ready + slack, now), -level[i], i)
                if best is None or key < best[0]:
                    best = key, ready
            (_, _, i), ready = best
            left.remove(i)
            name, deps, cost, fn, sends = self.tasks[i]
            start = max(ready, now)
            now = start + cost
            done[name] = now
            for event in sends:
                links, wire, hop = self.sends[event]
                begin = max([now, *(free.get(link, 0.0) for link in links)])
                for link in links:
                    free[link] = begin + wire
                done[event] = begin + wire + hop
            out.append((name, deps, fn, start))
        self.span = now
        return out


def kernel(
    both_ref, scale_ref, bias_ref, loss_ref, igrad_ref, tgrad_ref,
    IR, TR, CF, QI, OI, DI, TP, ZS, ZR, YS, YR, LS, LC, LX, LY, LZ,
    send_sem, recv_sem,
):
    img, txt = lax.axis_index("img"), lax.axis_index("txt")
    x, z, y, c = img // 8, img % 8, txt // 2, txt % 2

    def device(dx=0, dy=0, dz=0, dc=0):
        return (
            lax.rem(x + dx + 4, 4) * 8 + lax.rem(z + dz + 8, 8),
            lax.rem(y + dy + 4, 4) * 2 + lax.rem(c + dc, 2),
        )

    ways = {
        "x+": device(dx=1), "x-": device(dx=-1), "y+": device(dy=1), "y-": device(dy=-1),
        "z+": device(dz=1), "z-": device(dz=-1), "c": device(dc=1),
        "x2": device(dx=2), "y2": device(dy=2),
    }
    far = {("x", k): device(dx=k) for k in range(1, 4)}
    far |= {("y", k): device(dy=k) for k in range(1, 4)}
    far |= {("z", k): device(dz=k) for k in range(1, 8)}

    barrier = pltpu.get_barrier_semaphore()
    greeted = list(ways.values())
    for peer in greeted:
        pl.semaphore_signal(barrier, inc=1, device_id=peer, device_id_type=MESH)
    img_ref, txt_ref = both_ref.at[pl.ds(0, 64)], both_ref.at[pl.ds(64, 64)]
    scale = jnp.exp(jnp.full((1, 1), scale_ref[0], F32))
    offset = jnp.full((1, 1), bias_ref[0], F32)

    def unit(ref):
        wide = ref[...].astype(F32)
        norm = jnp.sqrt(jnp.sum(wide * wide, axis=1, keepdims=True) + 1e-06)
        return (wide / norm).astype(BF16)

    fixes = []
    for other in range(4):
        dz = lax.rem(c * 4 + other - z + 8, 8)
        core = lax.rem(z + c, 2)
        key = lax.rem(other - x + 4, 4) * 4 + lax.rem(x - y + 4, 4)
        slot = sum(jnp.where(key == i, PLACE[i // 4, i % 4], 0) for i in range(16))
        fixes.append((dz, dz * 128 + core * 64, slot * 64, (slot // 2) * 128, lax.rem(slot, 2) * 64))

    LS[...] = jnp.zeros_like(LS)
    IR[0:64, :] = unit(img_ref)
    TR[960:1024, :] = unit(txt_ref)
    pl.semaphore_wait(barrier, len(greeted))

    plan = Plan()
    copies, pending, boxes = {}, {}, {}

    def start(event, link, src, dst, sent):
        peer = ways[link] if isinstance(link, str) else far[link]
        key = plan.group.get(event, (event,))
        index = boxes.setdefault(key, len(boxes))
        out = pending.setdefault(sent, [len(pending), 0])
        out[1] += src.shape[0]
        copy = pltpu.make_async_remote_copy(
            src_ref=src, dst_ref=dst, send_sem=send_sem.at[out[0]], recv_sem=recv_sem.at[index],
            device_id=peer, device_id_type=MESH,
        )
        copy.start()
        copies[event] = copy, dst.shape[0]

    landed = set()

    def land(event):
        key = plan.group.get(event, (event,))
        if event not in plan.sends or key in landed:
            return
        landed.add(key)
        if len(key) == 1:
            copies[event][0].wait_recv()
            return
        rows = sum(copies[e][1] for e in key)
        ref = whole[event[0]].at[pl.ds(0, rows)]
        pltpu.make_async_copy(ref, ref, recv_sem.at[boxes[key]]).wait()

    whole = {"I": IR, "J": IR, "T": TR, "R": IR, "U": IR, "V": IR, "Lx": LZ, "Ly": LZ, "Lz": LZ}

    def forward(name, deps, moves):
        def run():
            for event, link, ref, here, there, rows in moves:
                start(event, link, ref.at[pl.ds(here, rows)], ref.at[pl.ds(there, rows)], "I" if ref is IR else "T")

        for event, link, _, _, _, rows in moves:
            plan.send(event, link, rows)
        plan.task(name, deps, 0.02 + 0.03 * len(moves), run, [m[0] for m in moves])

    def islot(dz, p):
        return dz * 128 + p * 16

    def image_move(dz, p, way):
        to = (dz - 1) % 8 if way == "z+" else (dz + 1) % 8
        return (("I", to, p), way, IR, islot(dz, p), islot(to, p), 16)

    def tslot(dx, dy, half, q=0):
        return PLACE[dx, dy] * 64 + half * 32 + q * 16

    def text_move(dx, dy, half, way, q):
        step = {"+": -1, "-": 1, "2": 2}[way[1]]
        ex = (dx + step) % 4 if way[0] == "x" else dx
        ey = (dy + step) % 4 if way[0] == "y" else dy
        event = ("T", ex, ey, half, q)
        return (event, way, TR, tslot(dx, dy, half, q), tslot(ex, ey, half, q), 16)

    plan.together(("I", 4, 0), ("I", 4, 1))
    plan.together(("I", 4, 2), ("I", 4, 3))
    plan.together(("J", 4, 0), ("J", 4, 1))
    plan.together(("I", 5, 2), ("I", 5, 3))
    plan.together(("I", 3, 0), ("I", 3, 1))
    for dz in (0, 2, 6):
        plan.together(("J", dz), ("J", dz + 1))
    for half in range(2):
        for a in range(4):
            places = [(a, b) if half == 0 else (b, a) for b in range(4)]
            plan.together(("T", *places[2], half, 0), ("T", *places[2], half, 1))
            if a in DIRECT:
                plan.together(("T", *places[1], half, 0), ("T", *places[1], half, 1))
                plan.together(("T", *places[3], half, 0), ("T", *places[3], half, 1))
            else:
                plan.together(("T", *places[1], half, 0), ("T", *places[3], half, 1))

    first = []
    for p in range(2):
        first += [image_move(0, p, "z+"), image_move(0, 3 - p, "z-")]
    for q in range(2):
        first += [text_move(0, 0, 0, w, q) for w in ("x+", "x-")]
        first += [text_move(0, 0, 1, w, q) for w in ("y+", "y-")]
    for p in range(2):
        first += [image_move(0, 2 + p, "z+"), image_move(0, 1 - p, "z-")]
    for q in range(2):
        first += [text_move(0, 0, 0, "x2", q), text_move(0, 0, 1, "y2", q)]
    for q in range(2):
        first += [text_move(0, 0, 0, w, q) for w in ("y+", "y-")]
        first += [text_move(0, 0, 1, w, q) for w in ("x+", "x-")]
    first += [(("J", 0), "c", IR, 0, 64, 64)]
    forward("first", [], first)
    for step in range(1, 4):
        for p in range(4 if step < 3 else 2):
            here = [("I", 8 - step, p), ("I", step, 3 - p)]
            plan.together(*here)
            moves = [image_move(8 - step, p, "z+"), image_move(step, 3 - p, "z-")]
            forward(("fI", step, p), here, moves)
    for dz in (1, 2, 3, 5, 6, 7):
        forward(
            ("fJ", dz), [("I", dz, p) for p in range(4)],
            [(("J", dz), "c", IR, dz * 128, dz * 128 + 64, 64)],
        )
    for k in range(2):
        forward(
            ("fJ", 4, k), [("I", 4, 2 * k), ("I", 4, 2 * k + 1)],
            [(("J", 4, k), "c", IR, 512 + k * 32, 576 + k * 32, 32)],
        )
    text_parts = {}
    for half in range(2):
        two = "y" if half == 0 else "x"

        def at(a, b, half=half):
            return (a, b) if half == 0 else (b, a)

        def mv(a, b, way, q, half=half, at=at):
            return text_move(*at(a, b), half, way, q)

        for a in range(4):
            for q in range(2):
                here = ("T", *at(a, 0), half, q)
                if a != 0:
                    moves = [mv(a, 0, two + "+", q), mv(a, 0, two + "-", q)]
                    if a in DIRECT:
                        moves.append(mv(a, 0, two + "2", q))
                    forward(("f1", half, a, q), [here], moves)
                if a in DIRECT:
                    continue
                b, way = ((3, "+"), (1, "-"))[q]
                forward(
                    ("f2", half, a, b), [("T", *at(a, b), half, q)], [mv(a, b, two + way, q)]
                )
            for b in range(4):
                names = [("T", *at(a, b), half, q) for q in range(2)]
                text_parts[(*at(a, b), half)] = names if (a, b) != (0, 0) else []
    image_parts = {dz: [*(("I", dz, p) for p in range(4)), ("J", dz)] for dz in range(8)}
    image_parts[0] = [("J", 0)]
    image_parts[4][-1:] = [("J", 4, 0), ("J", 4, 1)]

    def coef_block(r0, rows, c0, cols):
        acc = lax.dot_general(
            IR[r0 : r0 + rows, :], TR[c0 : c0 + cols, :], NT, preferred_element_type=F32
        )
        e = jnp.exp2(acc * (scale * LOG2E) + offset * LOG2E)
        d = 1.0 + e
        r = pltpu.reciprocal(d, approx=True)
        r = r * (2.0 - d * r)
        CF[r0 : r0 + rows, c0 : c0 + cols] = ((e * scale) * r).astype(BF16)
        w, h = cols // 2, rows // 2
        q = e[:, :w] * d[:, w:] + e[:, w:]
        q = q[:h] * (1.0 + q[h:]) + q[h:]
        u = 1.0 + q
        term = jnp.log(u) + (q - (u - 1.0)) * pltpu.reciprocal(u, approx=True)
        term = jnp.sum(term.reshape(h // 8, 8, w), axis=0)
        LS[...] += sum(term[:, k : k + 128] for k in range(0, w, 128))

    def diagonal(part):
        @pl.when(y == z // 2)
        def _():
            for dz, r0, t0, c0, shift in fixes:

                @pl.when(dz // 2 == part)
                def _(r0=r0, t0=t0, c0=c0, shift=shift):
                    r0 = pl.multiple_of(r0, 64)
                    t0 = pl.multiple_of(t0, 64)
                    c0 = pl.multiple_of(c0, 128)
                    pairs = IR[pl.ds(r0, 64), :].astype(F32) * TR[pl.ds(t0, 64), :].astype(F32)
                    logit = jnp.sum(pairs, axis=1, keepdims=True) * scale + offset
                    rows = lax.broadcasted_iota(jnp.int32, (64, 128), 0)
                    cols = lax.broadcasted_iota(jnp.int32, (64, 128), 1)
                    same = cols == rows + shift
                    mine = -scale / (1.0 + jnp.exp(logit))
                    block = CF[pl.ds(r0, 64), pl.ds(c0, 128)].astype(F32)
                    CF[pl.ds(r0, 64), pl.ds(c0, 128)] = jnp.where(same, mine, block).astype(BF16)
                    less = jnp.where(same, logit, 0.0)
                    LS[...] -= jnp.sum(less.reshape(8, 8, 128), axis=0)

    def text_ready(groups):
        deps = ["first"]
        for dx, dy in CHUNKS[4 * groups[0] : 4 * groups[-1] + 4]:
            deps += text_parts[dx, dy, 0] + text_parts[dx, dy, 1]
        return deps

    for pair in (0, 3, 1, 2):
        for group in (3, 2, 1, 0):
            plan.task(
                ("coef", pair, group),
                image_parts[2 * pair] + image_parts[2 * pair + 1] + text_ready((group,)), COEF_US,
                functools.partial(coef_block, pair * 256, 256, group * 256, 256),
            )
        plan.task(
            ("diag", pair), [("coef", pair, group) for group in range(4)], 0.1,
            functools.partial(diagonal, pair),
        )
    diagonals = [("diag", pair) for pair in range(4)]

    def spread(name, dep, value, box, place, links, events):
        def run():
            box[pl.ds(place, 1)] = value().reshape(1, 8, 128)
            for link, event in zip(links, events):
                start(event, link, box.at[pl.ds(place, 1)], box.at[pl.ds(place, 1)], name)

        plan.together(*events)
        for link, event in zip(links, events):
            plan.send(event, "tiny", 0)
        plan.task(name, dep, 0.1, run, events)

    spread("loss0", diagonals, lambda: LS[...], LC, c, ["c"], [("Lc", 1)])
    dep = [("Lc", 1)]
    for name, box, before, place, span in (("x", LX, LC, x, 4), ("y", LY, LX, y, 4), ("z", LZ, LY, z, 8)):
        links = [(name, k) for k in range(1, span)]
        events = [("L" + name, k) for k in range(1, span)]
        spread("loss" + name, dep, functools.partial(lambda b: jnp.sum(b[...], axis=0), before), box, place, links, events)
        dep = events

    def loss_end():
        loss_ref[0] = jnp.sum(jnp.sum(LZ[...], axis=0)) * (1.0 / TOTAL)

    plan.task("loss", dep, 0.1, loss_end)

    def image_group(pair):
        part = jnp.dot(
            CF[pair * 256 : pair * 256 + 256, :], TR[...], preferred_element_type=F32
        )
        for k in range(2):
            dz = 2 * pair + k
            QI[dz * 64 : dz * 64 + 64, :] = part[k * 128 : k * 128 + 64]
            OI[dz * 64 : dz * 64 + 64, :] = part[k * 128 + 64 : k * 128 + 128]
            rows = pl.ds(dz * 64, 64)
            start(("D", dz), "c", OI.at[rows], DI.at[rows], "D")

    def text_group(group):
        cols = slice(group * 256, group * 256 + 256)
        TP[cols, :] = lax.dot_general(CF[:, cols], IR[...], TN, preferred_element_type=F32)

    for dz in range(8):
        plan.send(("D", dz), "c", 128)
    for pair, group in ((2, 0), (1, 1), (3, 2), (0, 3)):
        plan.task(("TG", group), diagonals, 0.8, functools.partial(text_group, group))
        plan.task(
            ("G", pair), [("diag", pair)], 0.8, functools.partial(image_group, pair),
            [("D", 2 * pair), ("D", 2 * pair + 1)],
        )

    zplace = {}

    def zbox(box, way, dz, p):
        i = zplace.setdefault((way, dz, p), len(zplace))
        return box.at[pl.ds(i * 16, 16)]

    def run_all(parts):
        for work, _ in parts:
            work()
        for _, go in parts:
            go()

    def image_part(way, dz, p, arrived):
        def work():
            rows = slice(dz * 64 + p * 16, dz * 64 + p * 16 + 16)
            v = QI[rows, :] + DI[rows, :]
            if arrived:
                before = dz + 1 if way == "z+" else dz - 1
                v = v + decode(zbox(ZR, way, before, p)[...])
            zbox(ZS, way, dz, p)[...] = encode(v)

        def go():
            start(("R", way, dz, p), way, zbox(ZS, way, dz, p), zbox(ZR, way, dz, p), "R")

        return work, go

    ends = [("R", way, dz, p) for way, dz in (("z+", 1), ("z-", 7)) for p in range(4)]
    plan.together(*ends)
    for step in range(4):
        for p in range(4):
            if step == 0 and p > 1:
                continue
            arrived = step > 1 or (step == 1 and p < 2)
            near, away = ("z+", 4 - step, p), ("z-", 4 + step, 3 - p)
            deps = [("G", near[1] // 2), ("D", near[1]), ("G", away[1] // 2), ("D", away[1])]
            if arrived:
                deps += [("R", "z+", 5 - step, p), ("R", "z-", 3 + step, 3 - p)]
            events = [plan.send(("R", *near), "z+", 16), plan.send(("R", *away), "z-", 16)]
            if step < 3:
                plan.together(*events)
            parts = [image_part(*near, arrived), image_part(*away, arrived)]
            plan.task(("step", step, p), deps, STEP_US, functools.partial(run_all, parts), events)

    def project(emb_ref, rows, dgrad, out_ref):
        wide = emb_ref[rows, :].astype(F32)
        norm = jnp.sqrt(jnp.sum(wide * wide, axis=1, keepdims=True) + 1e-06)
        direction = wide / norm
        along = jnp.sum(direction * dgrad, axis=1, keepdims=True)
        out_ref[rows, :] = (dgrad - direction * along) / norm

    def image_end():
        for p in range(4):
            rows = slice(p * 16, p * 16 + 16)
            v = QI[rows, :] + DI[rows, :]
            v = v + decode(zbox(ZR, "z+", 1, p)[...]) + decode(zbox(ZR, "z-", 7, p)[...])
            project(img_ref, rows, v, igrad_ref)

    plan.task("image_end", [("G", 0), ("D", 0), *ends], 0.5, image_end)

    place = {}

    def ybox(box, key, rows):
        if key not in place:
            place[key] = sum(r for _, r in place.values()), rows
        return box.at[pl.ds(place[key][0], rows)]

    def take(event, rows):
        return decode(ybox(YR, event, rows)[...])

    def rows_of(half, a, b, q=None):
        start_row = tslot(b, a, half) if half == 0 else tslot(a, b, half)
        if q is None:
            return slice(start_row, start_row + 32)
        return slice(start_row + 16 * q, start_row + 16 * q + 16)

    def group(half, a, b):
        return ("TG", PLACE[(b, a) if half == 0 else (a, b)] // 4)

    def text_part(half, b, a, q, way, arrived):
        event = ("U", half, b, a, q)

        def work():
            v = TP[rows_of(half, a, b, q), :]
            if arrived:
                v = v + take(("U", half, b, 2, q), 16)
            ybox(YS, event, 16)[...] = encode(v)

        def go():
            start(event, way, ybox(YS, event, 16), ybox(YR, event, 16), "Y")

        return work, go

    def joined(half, b):
        parts = []
        for q in range(2):
            v = TP[rows_of(half, 0, b, q), :]
            for a in (1, 3):
                v = v + take(("U", half, b, a, q), 16)
            parts.append(v)
        return jnp.concatenate(parts, axis=0)

    def second_part(half, b, way):
        event = ("V", half, b)

        def work():
            ybox(YS, event, 32)[...] = encode(joined(half, b))

        def go():
            start(event, way, ybox(YS, event, 32), ybox(YR, event, 32), "Y")

        return work, go

    def text_end():
        for half in range(2):
            v = joined(half, 0)
            for b in (1, 2, 3):
                v = v + take(("V", half, b), 32)
            project(txt_ref, slice(half * 32, half * 32 + 32), v, tgrad_ref)

    one, two = ("y", "x"), ("x", "y")
    sides = ((1, "+"), (3, "-"))
    plan.together(*(("V", half, b) for half in range(2) for b in (1, 2, 3)))
    for b in (2, 1, 3, 0):
        outer, fresh, passed = [], [], []
        for half in range(2):
            for q, (a, sign) in enumerate(sides):
                outer.append((half, b, 2, q, one[half] + sign, False))
                fresh.append((half, b, a, 1 - q, one[half] + sign, False))
                passed.append((half, b, a, q, one[half] + sign, True))
        plan.together(*(("U", *part[:4]) for part in outer))
        plan.together(*(("U", *part[:4]) for part in fresh + passed))
        for kind, parts in (("outer", outer), ("fresh", fresh), ("passed", passed)):
            events = [plan.send(("U", *part[:4]), part[4], 16) for part in parts]
            deps = [group(part[0], part[2], b) for part in parts]
            if kind == "passed":
                deps += [("U", half, b, 2, q) for half in range(2) for q in range(2)]
            run = functools.partial(run_all, [text_part(*part) for part in parts])
            plan.task((kind, b), deps, 2 * STEP_US, run, events)
        base = [group(half, 0, b) for half in range(2)]
        base += [("U", *part[:4]) for part in fresh + passed]
        if b != 0:
            ways_two = [two[half] + {2: "2", 1: "+", 3: "-"}[b] for half in range(2)]
            events = [plan.send(("V", half, b), ways_two[half], 32) for half in range(2)]
            parts = [second_part(half, b, ways_two[half]) for half in range(2)]
            plan.task(("second", b), base, 0.25, functools.partial(run_all, parts), events)
        else:
            last = [("V", half, k) for half in range(2) for k in (1, 2, 3)]
            plan.task("text_end", [*base, *last], 0.5, text_end)

    for name, deps, fn, _ in plan.order():
        for event in deps:
            land(event)
        fn()
    for event in copies:
        land(event)
    sources = {"I": IR, "T": TR, "D": OI, "R": ZS, "Y": YS}
    for sent, (index, rows) in pending.items():
        ref = sources.get(sent, LZ).at[pl.ds(0, rows)]
        pltpu.make_async_copy(ref, ref, send_sem.at[index]).wait()


def per_device(image_emb, text_emb, log_scale, bias):
    width = image_emb.shape[1]
    vmem = pl.BlockSpec(memory_space=pltpu.VMEM)
    smem = pl.BlockSpec(memory_space=pltpu.SMEM)
    ring = 28 * 16
    return pl.pallas_call(
        kernel,
        out_shape=(
            jax.ShapeDtypeStruct((1,), F32),
            jax.ShapeDtypeStruct((64, width), F32),
            jax.ShapeDtypeStruct((64, width), F32),
        ),
        in_specs=[vmem, smem, smem],
        out_specs=(smem, vmem, vmem),
        scratch_shapes=[
            pltpu.VMEM((1024, width), BF16),
            pltpu.VMEM((1024, width), BF16),
            pltpu.VMEM((1024, 1024), BF16),
            pltpu.VMEM((512, width), F32),
            pltpu.VMEM((512, width), F32),
            pltpu.VMEM((512, width), F32),
            pltpu.VMEM((1024, width), F32),
            pltpu.VMEM((ring, width), BF16),
            pltpu.VMEM((ring, width), BF16),
            pltpu.VMEM((960, width), BF16),
            pltpu.VMEM((960, width), BF16),
            pltpu.VMEM((8, 128), F32),
            pltpu.VMEM((2, 8, 128), F32),
            pltpu.VMEM((4, 8, 128), F32),
            pltpu.VMEM((4, 8, 128), F32),
            pltpu.VMEM((8, 8, 128), F32),
            pltpu.SemaphoreType.DMA((9,)),
            pltpu.SemaphoreType.DMA((RECEIVED,)),
        ],
        compiler_params=pltpu.CompilerParams(
            collective_id=0, has_side_effects=True, vmem_limit_bytes=30 << 20
        ),
        cost_estimate=pl.CostEstimate(
            flops=6 * 1024 * 1024 * width, bytes_accessed=64 * width * 12, transcendentals=1 << 22
        ),
    )(jnp.concatenate([image_emb, text_emb], axis=0), log_scale, bias)


def solution(mesh):
    in_specs = (P(("img", "txt"), None), P(("txt", "img"), None), P(), P())
    out_specs = (P(), P(("img", "txt"), None), P(("txt", "img"), None))
    return jax.shard_map(
        per_device, mesh=mesh, in_specs=in_specs, out_specs=out_specs, check_vma=False
    )
```
